128 devices in a mesh: seq: 16 (over y, z), dec: 8 (over x, core).
Axes of the slice: x: 4, y: 4, z: 4, core: 2. Of those that a mesh axis runs over, the one named last changes fastest.
Arguments:
- query_nope: bfloat16 [8192, 16384], P('seq', 'dec'), may hold values from -6 to 6
- query_rope: bfloat16 [8192, 8192], P('seq', 'dec'), may hold values from -8 to 8
- latent_cache: bfloat16 [8192, 576], P(('seq', 'dec')), may hold values from -8 to 8
- key_up: bfloat16 [128, 128, 512], P('dec'), may hold values from -0.5 to 0.5
- value_up: bfloat16 [128, 512, 128], P('dec'), may hold values from -1 to 1
- vertical_lists: int32 [8, 256, 4], replicated, may hold values from 0 to 255, as said below
- page_owner: int32 [256, 1], replicated, may hold values from 0 to 7; in each aligned block of 16 rows (0 to 15, 16 to 31, ...) at most 3 rows name the same one
- step_nope: bfloat16 [64, 2, 16384], P('seq', None, 'dec'), may hold values from -6 to 6
- step_rope: bfloat16 [64, 2, 8192], P('seq', None, 'dec'), may hold values from -8 to 8
- step_latent: bfloat16 [64, 2, 576], P('seq'), may hold values from -6 to 6
- prefix_lengths: int32 [64], P('seq'), may hold values from 64 to 8192, as said below
Outputs:
- prefill_out: bfloat16 [8192, 16384], P('seq', 'dec')
- paged_cache: bfloat16 [8, 48, 32, 576], P('dec')
- decode_out: bfloat16 [64, 2, 16384], P('seq', None, 'dec')
The draws below stay inside these ranges and needn't reach their ends.
Inputs may be any that keep to these rules, and one draw needn't show every extreme that they name: `vertical_lists`: block numbers. The 64 entries of one head group for the query blocks of one seq index all differ; at most 1 of them name blocks k with the same k // 2, and 1 is reached. An entry may exceed its query block minus 3 only when no block at or before that limit can still be listed under the bound above; such entries are listed but not attended. `page_owner`: within the pages of one seq index (aligned blocks of 16 pages) no value appears more than 3 times, and 3 is reached. `prefix_lengths`: 8192 is reached.
All inputs are finite; a program needn't handle non-finite values.
Results may differ from the reference program's by a relative error of at most 0.0069.
Values may be sent and summed in bfloat16 or wider, within the bound.
A program may use at most 128 MiB of HBM per device.

```python
import math
import jax
import jax.numpy as jnp
import numpy as np
from jax import lax

HEADS = 128
NOPE = 128
ROPE = 64
LATENT = 512
VDIM = 128
BLK = 32
SLASH = 2
VB = 4
STEPS = 2
KVW = 576
SEQLEN = 8192
QB = 16
NQB = 256
HGRP = 16
KB = 2
CAP = 1
MOST = 3
SLOTS = 48
BATCH = 64
N_SEQ = 16
N_DEC = 8


def draw_query_rope(key, part):
    key = jax.random.fold_in(key, 1)
    values = jnp.clip(jax.random.normal(key, (SEQLEN, HEADS, ROPE), jnp.float32), -4.0, 4.0)
    return values.reshape(SEQLEN, HEADS * ROPE).astype(jnp.bfloat16)


def draw_latent_cache(key, part):
    key = jax.random.fold_in(key, 2)
    values = jnp.clip(jax.random.normal(key, (SEQLEN, LATENT + ROPE), jnp.float32), -4.0, 4.0)
    return values.astype(jnp.bfloat16)


def draw_step_rope(key, part):
    key = jax.random.fold_in(key, 3)
    values = jnp.clip(jax.random.normal(key, (BATCH, STEPS, HEADS, ROPE), jnp.float32), -4.0, 4.0)
    return values.reshape(BATCH, STEPS, HEADS * ROPE).astype(jnp.bfloat16)


def draw_vertical_lists(key, part):
    key = jax.random.fold_in(key, 4)
    holders = N_SEQ * N_DEC
    requests = QB * VB
    holder_ids = jnp.arange(holders, dtype=jnp.int32)

    def one_device(device_key, seq_position):

        def one_rank(rank_key):
            return jax.random.permutation(rank_key, holders)
        ranks = jax.vmap(one_rank)(jax.random.split(device_key, requests)).astype(jnp.int32)
        limits = (seq_position * QB + jnp.arange(requests, dtype=jnp.int32) // VB - SLASH - 1).astype(jnp.int32)

        def assign(counts, inputs):
            rank, limit = inputs
            candidate = holder_ids * KB + counts
            usable = counts < CAP
            attended = usable & (candidate <= limit)
            score = usable.astype(jnp.int32) * (4 * holders) + attended.astype(jnp.int32) * (2 * holders) + rank
            picked = jnp.argmax(score).astype(jnp.int32)
            chosen = picked * KB + counts[picked]
            counts = counts + (holder_ids == picked).astype(jnp.int32)
            return (counts, chosen)
        _, blocks = lax.scan(assign, jnp.zeros((holders,), jnp.int32), (ranks, limits))
        return blocks
    device_keys = jax.random.split(key, N_DEC * N_SEQ)
    seq_positions = jnp.tile(jnp.arange(N_SEQ, dtype=jnp.int32), N_DEC)
    blocks = jax.vmap(one_device)(device_keys, seq_positions)
    return blocks.reshape(N_DEC, NQB, VB).astype(jnp.int32)


def draw_prefix_lengths(key, part):
    key = jax.random.fold_in(key, 5)
    first_key, second_key = jax.random.split(key)
    lengths = jax.random.randint(first_key, (BATCH,), 2 * BLK, SEQLEN + 1, jnp.int32)
    chosen = jax.random.randint(second_key, (), 0, BATCH, jnp.int32)
    return jnp.where(jnp.arange(BATCH) == chosen, SEQLEN, lengths).astype(jnp.int32)


def level_of(rng, extent, shards, least, largest):
    loudness = 1.0
    for position, parts in shards:
        steps = jax.random.uniform(jax.random.fold_in(jax.random.fold_in(rng, 6), position), (parts,), jnp.float32, least / len(shards), largest / len(shards))
        loudness = loudness * jnp.repeat(jnp.exp(steps), extent[position] // parts).reshape((-1,) + (1,) * (len(extent) - 1 - position))
    return loudness


def deal_out(own_key, own, number, rows, number_of, top, most, slope):
    ranking = jax.random.permutation(own_key, number_of)
    packed, common = load_shares(number_of, rows * top, most, slope, True), load_shares(number_of, rows * top, most, slope, False)
    places = jnp.arange(number_of)

    def named(sizes, rotation):
        used = int((sizes > 0).sum())
        fixed = max(1, used // 4)
        shifted = fixed + (places - fixed + rotation * (used - fixed)) % max(1, number_of - fixed)
        return jnp.zeros((number_of,), jnp.int32).at[ranking[jnp.where(places < fixed, places, shifted)]].set(jnp.asarray(sizes, jnp.int32))

    sizes = jnp.where(number % 4 == 0, named(packed, number // 4), named(common, number - number // 4 - 1))
    mixed = jax.random.permutation(jax.random.fold_in(own, 3), number_of)
    source_of, sink = mixed[0:number_of // 2 * 2:2], mixed[1:number_of // 2 * 2:2]
    room = jnp.minimum(sizes[source_of] - 1, most - sizes[sink]) // 2
    room = jnp.where((source_of == ranking[0]) | (sink == ranking[0]) | (sizes[sink] == 0), 0, jnp.maximum(room, 0))
    shifted = jax.random.randint(jax.random.fold_in(own, 4), (number_of // 2,), 0, 1 << 20) % (room + 1)
    sizes = sizes.at[source_of].add(-shifted).at[sink].add(shifted)
    members = jnp.searchsorted(jnp.cumsum(sizes), jnp.arange(rows * top), side="right").astype(jnp.int32)
    listing = members.reshape(top, rows).T
    listing = listing[jax.random.permutation(jax.random.fold_in(own, 1), rows)]
    rotation = jax.random.randint(jax.random.fold_in(own, 2), (rows, 1), 0, top)
    return jnp.take_along_axis(listing, (jnp.arange(top)[None, :] + rotation) % top, axis=1)


def load_shares(count, total, most, slope, full):
    loads = [(1 << 20) // math.isqrt(rank ** slope) + 1 for rank in range(1, count + 1)]
    largest = most if full else min(most, max(-(-total // count), total * loads[0] // sum(loads)))
    least = 1 if total - largest >= count - 1 else 0
    given, surplus = [largest] + [least] * (count - 1), total - largest - least * (count - 1)
    while surplus > 0:
        candidates = [i for i in range(1, count) if given[i] < largest] or [i for i in range(1, count) if given[i] < most]
        mass, left = sum([loads[i] for i in candidates]), surplus
        for i in candidates:
            extra = min(most - given[i], max(1, left * loads[i] // mass), surplus)
            given[i] = given[i] + extra
            surplus = surplus - extra
    return np.array(given)


def centred(rng, dims, scale, most, cuts=(), kind=jnp.bfloat16):
    loudness = level_of(rng, dims, cuts, -0.22, 0.18) if cuts else 1.0
    entries = jax.random.normal(rng, dims, jnp.float32) * scale * loudness
    return jnp.minimum(jnp.maximum(entries, -most), most).astype(kind)


def setup_inputs(seed: int = 0) -> dict:
    splits = jax.random.split(jax.random.key(seed), 12)
    query_nope = centred(splits[0], (SEQLEN, HEADS * NOPE), 1.0, 6.0, ((0, 16), (1, 8)))
    query_rope = draw_query_rope(jax.random.fold_in(splits[11], 71), 0)
    latent_cache = draw_latent_cache(jax.random.fold_in(splits[11], 71), 0)
    key_up = centred(splits[3], (HEADS, NOPE, LATENT), NOPE ** -0.5, 0.5, ((0, 8),))
    value_up = centred(splits[4], (HEADS, LATENT, VDIM), (LATENT // 16) ** -0.5, 1.0, ((0, 8),))
    vertical_lists = draw_vertical_lists(jax.random.fold_in(splits[11], 71), 0)
    page_owner_keys = jax.random.split(jax.random.fold_in(splits[6], 1), NQB // QB)
    page_owner_turns = jax.random.permutation(jax.random.fold_in(splits[6], 3), NQB // QB)
    page_owner = jax.vmap(lambda own, number: deal_out(jax.random.fold_in(splits[6], 2), own, number, QB, N_DEC, 1, MOST, 2))(page_owner_keys, page_owner_turns).reshape((NQB, 1))
    step_nope = centred(splits[7], (BATCH, STEPS, HEADS * NOPE), 1.0, 6.0, ((0, 16), (2, 8)))
    step_rope = draw_step_rope(jax.random.fold_in(splits[11], 71), 0)
    step_latent = centred(splits[9], (BATCH, STEPS, KVW), 1.0, 6.0, ((0, 16),))
    prefix_lengths = draw_prefix_lengths(jax.random.fold_in(splits[11], 71), 0)
    return {"query_nope": query_nope, "query_rope": query_rope, "latent_cache": latent_cache, "key_up": key_up, "value_up": value_up, "vertical_lists": vertical_lists, "page_owner": page_owner, "step_nope": step_nope, "step_rope": step_rope, "step_latent": step_latent, "prefix_lengths": prefix_lengths}


def narrowed(values):
    return lax.optimization_barrier(values.astype(jnp.bfloat16)).astype(jnp.float32)


def softmax_masked(scores, allowed):
    masked = jnp.where(allowed, scores, -jnp.inf)
    highest = jnp.max(masked, axis=-1, keepdims=True)
    expval = jnp.where(allowed, jnp.exp(scores - highest), 0.0)
    return expval / jnp.sum(expval, axis=-1, keepdims=True)


def reference(query_nope, query_rope, latent_cache, key_up, value_up, vertical_lists, page_owner, step_nope, step_rope, step_latent, prefix_lengths):
    scale = float(NOPE + ROPE) ** -0.5
    width = LATENT + ROPE
    window = (SLASH + 1) * BLK
    key_up32 = key_up.astype(jnp.float32)
    value_up32 = value_up.astype(jnp.float32)
    latent32 = latent_cache.astype(jnp.float32)
    padded = jnp.concatenate([jnp.zeros((SLASH * BLK, width), jnp.float32), latent32], axis=0)
    key_blocks = latent32.reshape(NQB, BLK, width)
    row_index = jnp.arange(BLK, dtype=jnp.int32)
    window_index = jnp.arange(window, dtype=jnp.int32)

    def one_block(block_index):
        start = block_index * BLK
        nope_rows = lax.dynamic_slice_in_dim(query_nope, start, BLK, 0).reshape(BLK, HEADS, NOPE)
        rope_rows = lax.dynamic_slice_in_dim(query_rope, start, BLK, 0).reshape(BLK, HEADS, ROPE)
        absorbed = jnp.einsum("thn,hnc->thc", nope_rows.astype(jnp.float32), key_up32).astype(jnp.bfloat16)
        queries = jnp.concatenate([absorbed, rope_rows], axis=-1)
        queries = lax.optimization_barrier(queries).astype(jnp.float32).reshape(BLK, N_DEC, HGRP, width)
        slash_rows = lax.dynamic_slice_in_dim(padded, start, window, 0)
        picked = lax.dynamic_index_in_dim(vertical_lists, block_index, 1, keepdims=False)
        vertical = key_blocks[picked].reshape(N_DEC, VB * BLK, width)
        keys = jnp.concatenate([jnp.broadcast_to(slash_rows, (N_DEC, window, width)), vertical], axis=1)
        block_ok = (block_index - SLASH + window_index // BLK) >= 0
        causal = window_index[None, :] <= SLASH * BLK + row_index[:, None]
        slash_ok = jnp.broadcast_to((block_ok[None, :] & causal)[None], (N_DEC, BLK, window))
        vertical_ok = jnp.repeat(picked <= block_index - SLASH - 1, BLK, axis=1)
        vertical_ok = jnp.broadcast_to(vertical_ok[:, None, :], (N_DEC, BLK, VB * BLK))
        allowed = jnp.concatenate([slash_ok, vertical_ok], axis=2)
        scores = jnp.einsum("bghc,gkc->ghbk", queries, keys) * scale
        weights = narrowed(softmax_masked(scores, allowed[:, None]))
        context = jnp.einsum("ghbk,gkc->bghc", weights, keys[:, :, :LATENT])
        context = narrowed(context).reshape(BLK, HEADS, LATENT)
        values = jnp.einsum("bhc,hcv->bhv", context, value_up32).astype(jnp.bfloat16)
        return values.reshape(BLK, HEADS * VDIM)

    prefill_out = lax.map(one_block, jnp.arange(NQB, dtype=jnp.int32)).reshape(SEQLEN, HEADS * VDIM)

    owner_rows = page_owner[:, 0].reshape(N_SEQ, QB)
    owned = owner_rows[None] == jnp.arange(N_DEC, dtype=jnp.int32)[:, None, None]
    order = jnp.cumsum(owned.astype(jnp.int32), axis=2) - 1
    picks = owned[:, :, None, :] & (order[:, :, None, :] == jnp.arange(MOST, dtype=jnp.int32)[None, None, :, None])
    pages = latent32.reshape(N_SEQ, QB, BLK * width)
    paged = jnp.einsum("osmp,spx->osmx", picks.astype(jnp.float32), pages).astype(jnp.bfloat16)
    paged_cache = paged.reshape(N_DEC, SLOTS, BLK, width)

    positions = jnp.arange(SEQLEN, dtype=jnp.int32)
    step_index = jnp.arange(STEPS, dtype=jnp.int32)
    fresh_ok = (step_index[None, :] <= step_index[:, None])[:, None, :]

    def one_sequence(index):
        nope_rows = step_nope[index].reshape(STEPS, HEADS, NOPE).astype(jnp.float32)
        absorbed = jnp.einsum("shn,hnc->shc", nope_rows, key_up32).astype(jnp.bfloat16)
        queries = jnp.concatenate([absorbed, step_rope[index].reshape(STEPS, HEADS, ROPE)], axis=-1)
        queries = lax.optimization_barrier(queries).astype(jnp.float32)
        fresh = step_latent[index].astype(jnp.float32)
        cache_scores = jnp.einsum("shc,kc->shk", queries, latent32) * scale
        fresh_scores = jnp.einsum("shc,tc->sht", queries, fresh) * scale
        visible = (positions < prefix_lengths[index])[None, None, :]
        top = jnp.maximum(jnp.max(jnp.where(visible, cache_scores, -jnp.inf), axis=-1, keepdims=True), jnp.max(jnp.where(fresh_ok, fresh_scores, -jnp.inf), axis=-1, keepdims=True))
        cache_exp = jnp.where(visible, jnp.exp(cache_scores - top), 0.0)
        fresh_exp = jnp.where(fresh_ok, jnp.exp(fresh_scores - top), 0.0)
        numer = jnp.einsum("shk,kc->shc", narrowed(cache_exp), latent32[:, :LATENT]) + jnp.einsum("sht,tc->shc", narrowed(fresh_exp), fresh[:, :LATENT])
        denom = jnp.sum(cache_exp, axis=-1) + jnp.sum(fresh_exp, axis=-1)
        context = narrowed(numer / denom[..., None])
        values = jnp.einsum("shc,hcv->shv", context, value_up32).astype(jnp.bfloat16)
        return values.reshape(STEPS, HEADS * VDIM)

    decode_out = lax.map(one_sequence, jnp.arange(BATCH, dtype=jnp.int32))
    return prefill_out, paged_cache, decode_out
```

```python
import jax
import jax.numpy as jnp
from jax import lax
from jax.experimental import pallas as pl
from jax.experimental.pallas import tpu as pltpu
from jax.sharding import PartitionSpec as P

MESH = pl.DeviceIdType.MESH
ORDERS = (("x", "y", "z"), ("y", "z", "x"), ("z", "x", "y"))
ALL = slice(None)
COPIES = 200


class Gather:
    def __init__(self, cache, send, recv):
        seq, dec = lax.axis_index("seq"), lax.axis_index("dec")
        self.at = {"x": dec // 2, "y": seq // 4, "z": seq % 4}
        self.core = dec % 2
        self.cache, self.send, self.recv = cache, send, recv
        self.own = None
        self.sent, self.number, self.shares = [], {}, []

    def device(self, axis=None, by=0, mate=False):
        at = dict(self.at)
        if axis is not None:
            at[axis] = (at[axis] + by + 4) % 4
        core = 1 - self.core if mate else self.core
        return (at["y"] * 4 + at["z"], at["x"] * 2 + core)

    def slot(self, mate=False):
        core = 1 - self.core if mate else self.core
        return self.cache.at[self.at["y"], self.at["z"], self.at["x"], core]

    def chunk(self, g, rel, mate=False):
        where = []
        for axis in ("y", "z", "x"):
            r = rel[ORDERS[g].index(axis)]
            where.append(r if isinstance(r, slice) else (self.at[axis] + r + 4) % 4)
        core = 1 - self.core if mate else self.core
        return self.cache.at[where[0], where[1], where[2], core, pl.ds(6 * g, 6)]

    def copy(self, key, src, dst, target):
        k = self.number.setdefault(key, len(self.number))
        return pltpu.make_async_remote_copy(
            src_ref=src, dst_ref=dst, send_sem=self.send.at[k], recv_sem=self.recv.at[k],
            device_id=target, device_id_type=MESH)

    def hop(self, g, phase, rel, by):
        dst = self.chunk(g, rel)
        src = self.own.at[pl.ds(6 * g, 6)] if rel == (0, 0, 0) else dst
        key = (g, phase) + tuple(map(str, rel)) + (by,)
        copy = self.copy(key, src, dst, self.device(ORDERS[g][phase], by))
        copy.start()
        self.sent.append(copy)

    def land(self, g, phase, rel, by):
        got = list(rel)
        got[phase] = {0: -by, -by: 2}[rel[phase]]
        if got[phase] == -2:
            got[phase] = 2
        dst = self.chunk(g, got)
        key = (g, phase) + tuple(map(str, rel)) + (by,)
        self.copy(key, dst, dst, self.device(mate=True)).wait_recv()
        return tuple(got)

    def give(self, g, rel):
        src = self.chunk(g, rel)
        key = ("core", g) + tuple(map(str, rel))
        copy = self.copy(key, src, src, self.device(mate=True))
        copy.start()
        self.sent.append(copy)
        self.shares.append((key, self.chunk(g, rel, mate=True)))

    def give_own(self):
        copy = self.copy(("core",), self.own, self.slot(), self.device(mate=True))
        copy.start()
        self.sent.append(copy)
        self.shares.append((("core",), self.slot(mate=True)))

    def take(self):
        for key, ref in self.shares:
            self.copy(key, ref, ref, self.device(mate=True)).wait_recv()

    def barrier_start(self):
        sem = pltpu.get_barrier_semaphore()
        for axis in ("x", "y", "z"):
            for by in (-1, 1, 2):
                pl.semaphore_signal(sem, inc=1, device_id=self.device(axis, by), device_id_type=MESH)
        pl.semaphore_signal(sem, inc=1, device_id=self.device(mate=True), device_id_type=MESH)

    def barrier_wait(self):
        pl.semaphore_wait(pltpu.get_barrier_semaphore(), 10)

    def steps(self):
        three = range(3)
        near = (1, -1)
        for phase in (0, 1):
            for g in three:
                for by in near + (2,):
                    self.hop(g, phase, (0, 0, 0), by)
        for g in three:
            for by in near:
                self.hop(g, 2, (0, 0, 0), by)
        self.give_own()
        yield "own"
        for by in near + (2,):
            for g in three:
                got = self.land(g, 0, (0, 0, 0), by)
                for way in near + (2,):
                    self.hop(g, 1, got, way)
            yield "first"
        for by in near + (2,):
            for g in three:
                got = (-by if by != 2 else 2, 0, 0)
                for way in near:
                    self.hop(g, 2, got, way)
                self.give(g, got)
        yield "first"
        for by in near + (2,):
            for g in three:
                for r1 in (0, 1, -1, 2):
                    got = self.land(g, 1, (r1, 0, 0), by)
                got = (ALL,) + got[1:]
                for way in near:
                    self.hop(g, 2, got, way)
                self.give(g, got)
            yield "second"
        for g in three:
            for r1, on in ((0, 1), (1, -1), (-1, 1), (2, -1)):
                for by in near:
                    got = self.land(g, 2, (r1, 0, 0), by)
                    if by == on:
                        self.hop(g, 2, got, by)
            for r3 in near:
                self.give(g, (ALL, 0, r3))
            yield "third"
        for r2 in near + (2,):
            for g in three:
                for by in near:
                    got = self.land(g, 2, (ALL, r2, 0), by)
                    if r2 == 2:
                        self.hop(g, 2, (slice(0, 2) if by == 1 else slice(2, 4),) + got[1:], by)
                    elif r2 == by:
                        self.hop(g, 2, got, by)
                    self.give(g, got)
                yield "third"
        for g in three:
            for r1, on in ((0, 1), (1, -1), (-1, 1), (2, -1)):
                self.land(g, 2, (r1, 0, -on), on)
            self.give(g, (ALL, 0, 2))
        yield "far"
        for r2 in near:
            for g in three:
                self.give(g, self.land(g, 2, (ALL, r2, -r2), r2))
            yield "far"
        for g in three:
            self.land(g, 2, (slice(0, 2), 2, -1), 1)
            self.land(g, 2, (slice(2, 4), 2, 1), -1)
            self.give(g, (ALL, 2, 2))
        yield "far"
        self.take()
        for copy in self.sent:
            copy.wait_send()
        yield "all"


BLK = 32
VB = 4
SLASH = 2
TILES = 9
HALF = 8
SCALE = 192.0 ** -0.5
EXP2 = SCALE * 1.4426950408889634
NEG = float("-inf")


def dot(a, b):
    return jnp.dot(a, b, preferred_element_type=jnp.float32)


def dot_t(a, b):
    return lax.dot_general(a, b, (((1,), (1,)), ((), ())), preferred_element_type=jnp.float32)


def even_first(h):
    return (h % 2) * HALF + h // 2


def pack(rows, tiles):
    for b in range(2):
        for r in range(2):
            start = 32 * b + 16 * r
            for c in range(4):
                tiles[9 * b + 4 * r + c] = rows[start : start + 16, 128 * c : 128 * c + 128]
        tiles[9 * b + 8] = jnp.concatenate(
            [rows[32 * b : 32 * b + 16, 512:576], rows[32 * b + 16 : 32 * b + 32, 512:576]], axis=1
        )


def rope_pair(tile):
    swapped = jnp.concatenate([tile[..., 64:], tile[..., :64]], axis=-1)
    low = lax.broadcasted_iota(jnp.int32, tile.shape, tile.ndim - 1) < 64
    zero = jnp.zeros_like(tile)
    first = (jnp.where(low, tile, zero), jnp.where(low, swapped, zero))
    second = (jnp.where(low, zero, swapped), jnp.where(low, zero, tile))
    return first, second


def gather_kernel(
    prefix, latent, step_nope, step_rope, step_latent, query_nope, key_up,
    cache, absorbed, decoded,
    tiles, qn, ku, hold, chunk, keys, rope, dq, dr, acc, top, total,
    send, recv, local, held, loaded,
):
    t = Gather(cache, send, recv)
    t.barrier_start()
    in_q = pltpu.make_async_copy(query_nope, qn, local.at[0])
    in_k = pltpu.make_async_copy(key_up, ku, local.at[1])
    in_q.start()
    in_k.start()
    pack(latent, tiles)
    t.barrier_wait()
    t.own = tiles
    own_copy = pltpu.make_async_copy(tiles, t.slot(), local.at[2])
    own_copy.start()

    copies = [None, None]

    def absorb(h):
        if h == 0:
            in_q.wait()
            in_k.wait()
        slot = h % 2
        if copies[slot] is not None:
            copies[slot].wait()
        got = dot(qn[:, 128 * h : 128 * h + 128], ku[h]).astype(jnp.bfloat16)
        hold[slot] = got.reshape(16, BLK, 512)
        copies[slot] = pltpu.make_async_copy(hold.at[slot], absorbed.at[:, even_first(h)], held.at[slot])
        copies[slot].start()

    def decode_start():
        for p in range(HALF):
            for odd in range(2):
                h = 2 * p + odd
                dq[odd, p] = dot(step_nope[:, 128 * h : 128 * h + 128], ku[h])
            dr[p] = step_rope[:, 128 * p : 128 * p + 128].astype(jnp.float32)
        q = dq[...].reshape(128, 512).astype(jnp.bfloat16)
        r = dr[...].reshape(64, 128).astype(jnp.bfloat16)
        fresh = step_latent[...]
        fr = fresh[:, 512:576]
        zero = jnp.zeros((8, 64), jnp.bfloat16)
        even = dot_t(r, jnp.concatenate([fr, zero], axis=1))
        odd = dot_t(r, jnp.concatenate([zero, fr], axis=1))
        s = dot_t(q, fresh[:, :512]) + jnp.concatenate([even, odd], axis=0)
        row = lax.broadcasted_iota(jnp.int32, (128, 8), 0) % 8
        key = lax.broadcasted_iota(jnp.int32, (128, 8), 1)
        s = jnp.where((row // 2 == key // 2) & (key <= row), s, NEG)
        m = jnp.max(s, axis=1, keepdims=True)
        e = jnp.exp2((s - m) * EXP2)
        top[...] = jnp.broadcast_to(m, (128, 128))
        total[...] = jnp.broadcast_to(jnp.sum(e, axis=1, keepdims=True), (128, 128))
        acc[...] = dot(e.astype(jnp.bfloat16), fresh[:, :512])

    def load(n):
        return pltpu.make_async_copy(cache.at[n // 4, n % 4], chunk.at[n % 2], loaded.at[n % 2])

    def decode(n):
        for x in range(4):
            for c in range(2):
                for b in range(2):
                    blk = (x * 2 + c) * 2 + b
                    for r in range(2):
                        at = 32 * blk + 16 * r
                        for w in range(4):
                            keys[at : at + 16, 128 * w : 128 * w + 128] = chunk[n % 2, x, c, 9 * b + 4 * r + w]
                    first, second = rope_pair(chunk[n % 2, x, c, 9 * b + 8])
                    for r in range(2):
                        at = 32 * blk + 16 * r
                        rope[0, at : at + 16] = first[r]
                        rope[1, at : at + 16] = second[r]
        q = dq[...].reshape(128, 512).astype(jnp.bfloat16)
        r = dr[...].reshape(64, 128).astype(jnp.bfloat16)
        s = dot_t(q, keys[...]) + jnp.concatenate([dot_t(r, rope[0]), dot_t(r, rope[1])], axis=0)
        row = lax.broadcasted_iota(jnp.int32, (128, 512), 0) % 8 // 2
        limit = jnp.where(row == 0, prefix[0], jnp.where(row == 1, prefix[1], jnp.where(row == 2, prefix[2], prefix[3])))
        place = lax.broadcasted_iota(jnp.int32, (128, 512), 1) + 512 * n
        s = jnp.where(place < limit, s, NEG)
        before = top[:, :1]
        m = jnp.maximum(before, jnp.max(s, axis=1, keepdims=True))
        keep = jnp.exp2((before - m) * EXP2)
        e = jnp.exp2((s - m) * EXP2)
        top[...] = jnp.broadcast_to(m, (128, 128))
        total[...] = total[...] * keep + jnp.sum(e, axis=1, keepdims=True)
        acc[...] = acc[...] * keep + dot(e.astype(jnp.bfloat16), keys[...])

    step = 0
    for name in t.steps():
        if step < 8:
            absorb(2 * step)
            absorb(2 * step + 1)
        elif step == 8:
            decode_start()
        step += 1
    own_copy.wait()
    for c in copies:
        c.wait()
    load(0).start()
    for n in range(16):
        if n < 15:
            load(n + 1).start()
        load(n).wait()
        decode(n)
    decoded[...] = (acc[...] / total[:, :1]).reshape(2, HALF, 8, 512)


def attend_kernel(
    listed, slots, cache, absorbed, query_rope, value_up, decoded,
    prefill_out, paged, decode_out,
    near, far, qa, qr, vu, pages, keys, rope, ctx, out, paged_hold,
    s_near, s_far, s_qa, s_in, s_page, s_out, s_paged,
):
    seq = lax.axis_index("seq")
    own = [
        pltpu.make_async_copy(cache.at[pl.ds(seq * 16, 16)], near.at[pl.ds(2, 16)], s_near.at[0]),
        pltpu.make_async_copy(cache.at[pl.ds(jnp.maximum(seq * 16 - 2, 0), 2)], near.at[pl.ds(0, 2)], s_near.at[1]),
        pltpu.make_async_copy(query_rope, qr, s_in.at[0]),
    ]

    def far_copy(i):
        return pltpu.make_async_copy(cache.at[listed[i]], far.at[i], s_far.at[i])

    def qa_copy(n):
        return pltpu.make_async_copy(absorbed.at[n], qa.at[n], s_qa.at[n])

    def page_copy(i):
        return pltpu.make_async_copy(cache.at[jnp.maximum(slots[i], 0)], pages.at[i], s_page.at[i])

    for c in own:
        c.start()
    for n in range(16):
        qa_copy(n).start()
        for v in range(VB):
            far_copy(n * VB + v).start()
    in_vu = pltpu.make_async_copy(value_up, vu, s_in.at[1])
    in_vu.start()

    @pl.loop(0, 48)
    def _(i):
        page_copy(i).start()

    keys[224:256] = jnp.zeros((32, 512), jnp.bfloat16)
    rope[:, 224:256] = jnp.zeros((2, 32, 128), jnp.bfloat16)
    for c in own:
        c.wait()

    def place(block, at):
        for r in range(2):
            for w in range(4):
                keys[at + 16 * r : at + 16 * r + 16, 128 * w : 128 * w + 128] = block[4 * r + w]
        first, second = rope_pair(block[8])
        for r in range(2):
            rope[0, at + 16 * r : at + 16 * r + 16] = first[r]
            rope[1, at + 16 * r : at + 16 * r + 16] = second[r]

    @pl.loop(0, 16)
    def _(n):
        qa_copy(n).wait()
        col = lax.broadcasted_iota(jnp.int32, (BLK, 256), 1)
        row = lax.broadcasted_iota(jnp.int32, (BLK, 256), 0)
        here = seq * 16 + n
        ok = (col >= 128) & (col - 128 <= SLASH * BLK + row) & (here - SLASH + (col - 128) // BLK >= 0)
        for v in range(VB):
            far_copy(n * VB + v).wait()
            place(far[n * VB + v], BLK * v)
            listed_here = listed[n * VB + v] <= here - SLASH - 1
            ok = ok | ((col // BLK == v) & listed_here)
        for v in range(SLASH + 1):
            place(near[n + v], 128 + BLK * v)
        bias = jnp.where(ok, 0.0, NEG)
        q = qa[n].reshape(512, 512)
        start = pl.multiple_of(n * BLK, BLK)
        r = jnp.concatenate([qr[pl.ds(start, BLK), 128 * p : 128 * p + 128] for p in range(HALF)], axis=0)
        s = dot_t(q, keys[...]) + jnp.concatenate([dot_t(r, rope[0]), dot_t(r, rope[1])], axis=0)
        s = (s.reshape(16, BLK, 256) + bias[None]).reshape(512, 256)
        m = jnp.max(s, axis=1, keepdims=True)
        e = jnp.exp2((s - m) * EXP2)
        total = jnp.sum(e, axis=1, keepdims=True)
        got = dot(e.astype(jnp.bfloat16), keys[...]) / total
        ctx[:, pl.ds(start, BLK), :] = got.astype(jnp.bfloat16).reshape(16, BLK, 512)
        for j in range(3):
            i = 3 * n + j
            page_copy(i).wait()
            page = pages[i]
            page = jnp.where(slots[i] >= 0, page, jnp.zeros_like(page))
            for r2 in range(2):
                rows = slice(16 * r2, 16 * r2 + 16)
                for w in range(4):
                    paged_hold[i, rows, 128 * w : 128 * w + 128] = page[4 * r2 + w]
                paged_hold[i, rows, 512:576] = page[8][:, 64 * r2 : 64 * r2 + 64]

    out_paged = pltpu.make_async_copy(paged_hold, paged.at[0], s_paged)
    out_paged.start()
    in_vu.wait()
    outs = []
    for h in range(16):
        i = even_first(h)
        cols = slice(128 * h, 128 * h + 128)
        out[:, cols] = dot(ctx[i], vu[h]).astype(jnp.bfloat16)
        got = dot(decoded[h % 2, h // 2].astype(jnp.bfloat16), vu[h]).astype(jnp.bfloat16)
        for b in range(4):
            decode_out[b, :, cols] = got[2 * b : 2 * b + 2]
        if h % 4 == 3:
            wide = slice(128 * (h - 3), 128 * h + 128)
            copy = pltpu.make_async_copy(out.at[:, wide], prefill_out.at[:, wide], s_out.at[h // 4])
            copy.start()
            outs.append(copy)
    for copy in outs:
        copy.wait()
    out_paged.wait()


def on_device(
    query_nope, query_rope, latent_cache, key_up, value_up, vertical_lists, page_owner,
    step_nope, step_rope, step_latent, prefix_lengths,
):
    seq, dec = lax.axis_index("seq"), lax.axis_index("dec")
    vmem, smem, any_ = (pl.BlockSpec(memory_space=m) for m in (pltpu.VMEM, pltpu.SMEM, pl.ANY))
    bf16, f32 = jnp.bfloat16, jnp.float32
    dma = pltpu.SemaphoreType.DMA
    cache, absorbed, decoded = pl.pallas_call(
        gather_kernel,
        out_shape=(
            jax.ShapeDtypeStruct((4, 4, 4, 2, 18, 16, 128), bf16),
            jax.ShapeDtypeStruct((16, 16, BLK, 512), bf16),
            jax.ShapeDtypeStruct((2, HALF, 8, 512), f32),
        ),
        in_specs=[smem, vmem, vmem, vmem, vmem, any_, any_],
        out_specs=(any_, any_, vmem),
        scratch_shapes=[
            pltpu.VMEM((18, 16, 128), bf16),
            pltpu.VMEM((512, 2048), bf16),
            pltpu.VMEM((16, 128, 512), bf16),
            pltpu.VMEM((2, 16, BLK, 512), bf16),
            pltpu.VMEM((2, 4, 2, 18, 16, 128), bf16),
            pltpu.VMEM((512, 512), bf16),
            pltpu.VMEM((2, 512, 128), bf16),
            pltpu.VMEM((2, HALF, 8, 512), f32),
            pltpu.VMEM((HALF, 8, 128), f32),
            pltpu.VMEM((128, 512), f32),
            pltpu.VMEM((128, 128), f32),
            pltpu.VMEM((128, 128), f32),
            dma((COPIES,)), dma((COPIES,)), dma((3,)), dma((2,)), dma((2,)),
        ],
        compiler_params=pltpu.CompilerParams(
            collective_id=0, has_side_effects=True, vmem_limit_bytes=56 << 20
        ),
        cost_estimate=pl.CostEstimate(flops=4 << 30, bytes_accessed=32 << 20, transcendentals=1 << 20),
        name="gather_absorb_decode",
    )(
        prefix_lengths, latent_cache, step_nope.reshape(8, 2048), step_rope.reshape(8, 1024),
        step_latent.reshape(8, 576), query_nope, key_up,
    )
    listed = lax.dynamic_slice(vertical_lists, (dec, seq * 16, 0), (1, 16, VB)).reshape(64)
    owned = page_owner.reshape(16, 16) == dec
    rank = jnp.cumsum(owned.astype(jnp.int32), axis=1) - 1
    picks = owned[:, None, :] & (rank[:, None, :] == jnp.arange(3)[None, :, None])
    number = jnp.arange(256).reshape(16, 1, 16)
    slots = jnp.max(jnp.where(picks, number, -1), axis=2).reshape(48)
    prefill_out, paged, decode_out = pl.pallas_call(
        attend_kernel,
        out_shape=(
            jax.ShapeDtypeStruct((512, 2048), bf16),
            jax.ShapeDtypeStruct((1, 48, BLK, 576), bf16),
            jax.ShapeDtypeStruct((4, 2, 2048), bf16),
        ),
        in_specs=[smem, smem, any_, any_, any_, any_, vmem],
        out_specs=(any_, any_, vmem),
        scratch_shapes=[
            pltpu.VMEM((18, TILES, 16, 128), bf16),
            pltpu.VMEM((64, TILES, 16, 128), bf16),
            pltpu.VMEM((16, 16, BLK, 512), bf16),
            pltpu.VMEM((512, 1024), bf16),
            pltpu.VMEM((16, 512, 128), bf16),
            pltpu.VMEM((48, TILES, 16, 128), bf16),
            pltpu.VMEM((256, 512), bf16),
            pltpu.VMEM((2, 256, 128), bf16),
            pltpu.VMEM((16, 512, 512), bf16),
            pltpu.VMEM((512, 2048), bf16),
            pltpu.VMEM((48, BLK, 576), bf16),
            dma((2,)), dma((64,)), dma((16,)), dma((2,)), dma((48,)), dma((4,)), dma,
        ],
        compiler_params=pltpu.CompilerParams(vmem_limit_bytes=56 << 20),
        cost_estimate=pl.CostEstimate(flops=6 << 30, bytes_accessed=20 << 20, transcendentals=2 << 20),
        name="attend",
    )(listed, slots, cache.reshape(256, TILES, 16, 128), absorbed, query_rope, value_up, decoded)
    return prefill_out, paged, decode_out


def solution(mesh):
    placed = (
        P("seq", "dec"), P("seq", "dec"), P(("seq", "dec"), None), P("dec", None, None), P("dec", None, None),
        P(), P(), P("seq", None, "dec"), P("seq", None, "dec"), P("seq", None, None), P("seq"),
    )
    return jax.shard_map(
        on_device,
        mesh=mesh,
        in_specs=placed,
        out_specs=(P("seq", "dec"), P("dec", None, None, None), P("seq", None, "dec")),
        check_vma=False,
    )
```

```python
import jax
import jax.numpy as jnp
from jax import lax
from jax.experimental import pallas as pl
from jax.experimental.pallas import tpu as pltpu
from jax.sharding import PartitionSpec as P

MESH = pl.DeviceIdType.MESH
ORDERS = (("x", "y", "z"), ("y", "z", "x"), ("z", "x", "y"))
ALL = slice(None)
COPIES = 200


class Gather:
    def __init__(self, cache, send, recv):
        seq, dec = lax.axis_index("seq"), lax.axis_index("dec")
        self.at = {"x": dec // 2, "y": seq // 4, "z": seq % 4}
        self.core = dec % 2
        self.cache, self.send, self.recv = cache, send, recv
        self.own = None
        self.sent, self.number, self.shares = [], {}, []

    def device(self, axis=None, by=0, mate=False):
        at = dict(self.at)
        if axis is not None:
            at[axis] = (at[axis] + by + 4) % 4
        core = 1 - self.core if mate else self.core
        return (at["y"] * 4 + at["z"], at["x"] * 2 + core)

    def slot(self, mate=False):
        core = 1 - self.core if mate else self.core
        return self.cache.at[self.at["y"], self.at["z"], self.at["x"], core]

    def chunk(self, g, rel, mate=False):
        where = []
        for axis in ("y", "z", "x"):
            r = rel[ORDERS[g].index(axis)]
            where.append(r if isinstance(r, slice) else (self.at[axis] + r + 4) % 4)
        core = 1 - self.core if mate else self.core
        return self.cache.at[where[0], where[1], where[2], core, pl.ds(6 * g, 6)]

    def copy(self, key, src, dst, target):
        k = self.number.setdefault(key, len(self.number))
        return pltpu.make_async_remote_copy(
            src_ref=src, dst_ref=dst, send_sem=self.send.at[k], recv_sem=self.recv.at[k],
            device_id=target, device_id_type=MESH)

    def hop(self, g, phase, rel, by):
        dst = self.chunk(g, rel)
        src = self.own.at[pl.ds(6 * g, 6)] if rel == (0, 0, 0) else dst
        key = (g, phase) + tuple(map(str, rel)) + (by,)
        copy = self.copy(key, src, dst, self.device(ORDERS[g][phase], by))
        copy.start()
        self.sent.append(copy)

    def land(self, g, phase, rel, by):
        got = list(rel)
        got[phase] = {0: -by, -by: 2}[rel[phase]]
        if got[phase] == -2:
            got[phase] = 2
        dst = self.chunk(g, got)
        key = (g, phase) + tuple(map(str, rel)) + (by,)
        self.copy(key, dst, dst, self.device(mate=True)).wait_recv()
        return tuple(got)

    def give(self, g, rel):
        src = self.chunk(g, rel)
        key = ("core", g) + tuple(map(str, rel))
        copy = self.copy(key, src, src, self.device(mate=True))
        copy.start()
        self.sent.append(copy)
        self.shares.append((key, self.chunk(g, rel, mate=True)))

    def give_own(self):
        copy = self.copy(("core",), self.own, self.slot(), self.device(mate=True))
        copy.start()
        self.sent.append(copy)
        self.shares.append((("core",), self.slot(mate=True)))

    def take(self):
        for key, ref in self.shares:
            self.copy(key, ref, ref, self.device(mate=True)).wait_recv()

    def barrier_start(self):
        sem = pltpu.get_barrier_semaphore()
        for axis in ("x", "y", "z"):
            for by in (-1, 1, 2):
                pl.semaphore_signal(sem, inc=1, device_id=self.device(axis, by), device_id_type=MESH)
        pl.semaphore_signal(sem, inc=1, device_id=self.device(mate=True), device_id_type=MESH)

    def barrier_wait(self):
        pl.semaphore_wait(pltpu.get_barrier_semaphore(), 10)

    def steps(self):
        three = range(3)
        near = (1, -1)
        for phase in (0, 1):
            for g in three:
                for by in near + (2,):
                    self.hop(g, phase, (0, 0, 0), by)
        for g in three:
            for by in near:
                self.hop(g, 2, (0, 0, 0), by)
        self.give_own()
        yield "own"
        for by in near + (2,):
            for g in three:
                got = self.land(g, 0, (0, 0, 0), by)
                for way in near + (2,):
                    self.hop(g, 1, got, way)
            yield "first"
        for by in near + (2,):
            for g in three:
                got = (-by if by != 2 else 2, 0, 0)
                for way in near:
                    self.hop(g, 2, got, way)
                self.give(g, got)
        yield "first"
        for by in near + (2,):
            for g in three:
                for r1 in (0, 1, -1, 2):
                    got = self.land(g, 1, (r1, 0, 0), by)
                got = (ALL,) + got[1:]
                for way in near:
                    self.hop(g, 2, got, way)
                self.give(g, got)
            yield "second"
        for g in three:
            for r1, on in ((0, 1), (1, -1), (-1, 1), (2, -1)):
                for by in near:
                    got = self.land(g, 2, (r1, 0, 0), by)
                    if by == on:
                        self.hop(g, 2, got, by)
            for r3 in near:
                self.give(g, (ALL, 0, r3))
            yield "third"
        for r2 in near + (2,):
            for g in three:
                for by in near:
                    got = self.land(g, 2, (ALL, r2, 0), by)
                    if r2 == 2:
                        self.hop(g, 2, (slice(0, 2) if by == 1 else slice(2, 4),) + got[1:], by)
                    elif r2 == by:
                        self.hop(g, 2, got, by)
                    self.give(g, got)
                yield "third"
        for g in three:
            for r1, on in ((0, 1), (1, -1), (-1, 1), (2, -1)):
                self.land(g, 2, (r1, 0, -on), on)
            self.give(g, (ALL, 0, 2))
        yield "far"
        for r2 in near:
            for g in three:
                self.give(g, self.land(g, 2, (ALL, r2, -r2), r2))
            yield "far"
        for g in three:
            self.land(g, 2, (slice(0, 2), 2, -1), 1)
            self.land(g, 2, (slice(2, 4), 2, 1), -1)
            self.give(g, (ALL, 2, 2))
        yield "far"
        self.take()
        for copy in self.sent:
            copy.wait_send()
        yield "all"


BLK = 32
VB = 4
SLASH = 2
UNROLL = 4
EXP2 = 192.0 ** -0.5 * 1.4426950408889634
NEG = float("-inf")


def dot(a, b):
    return jnp.dot(a, b, preferred_element_type=jnp.float32)


def dot_t(a, b):
    return lax.dot_general(a, b, (((1,), (1,)), ((), ())), preferred_element_type=jnp.float32)


def pack(rows, tiles):
    for b in range(2):
        for r in range(2):
            start = 32 * b + 16 * r
            for c in range(4):
                tiles[9 * b + 4 * r + c] = rows[start : start + 16, 128 * c : 128 * c + 128]
        tiles[9 * b + 8] = jnp.concatenate(
            [rows[32 * b : 32 * b + 16, 512:576], rows[32 * b + 16 : 32 * b + 32, 512:576]], axis=1
        )


def keys_from(blocks):
    n = blocks.shape[0]

    def rows(first, second):
        return jnp.stack([first, second], axis=1).reshape(n * BLK, 128)

    latent = jnp.concatenate([rows(blocks[:, w], blocks[:, 4 + w]) for w in range(4)], axis=1)
    tile = blocks[:, 8]
    low = lax.broadcasted_iota(jnp.int32, tile.shape, 2) < 64
    zero = jnp.zeros_like(tile)
    return latent, rows(jnp.where(low, tile, zero), jnp.where(low, zero, tile))


def gather_kernel(
    prefix, latent, step_nope, step_rope, step_latent, query_nope, query_rope, key_up,
    cache, absorbed, decoded,
    tiles, qn, qr, ku, dq, acc, top, total,
    send, recv, local,
):
    t = Gather(cache, send, recv)
    t.barrier_start()
    loads = [
        pltpu.make_async_copy(src, dst, local.at[i])
        for i, (src, dst) in enumerate(((query_nope, qn), (key_up, ku), (query_rope, qr)))
    ]
    for c in loads:
        c.start()
    pack(latent, tiles)
    t.own = tiles
    t.barrier_wait()
    own_copy = pltpu.make_async_copy(tiles, t.slot(), local.at[3])
    own_copy.start()

    def absorb(h):
        got = dot(qn[:, 128 * h : 128 * h + 128], ku[h]).astype(jnp.bfloat16)
        absorbed[:, h, :, :512] = got.reshape(16, BLK, 512)
        rope = qr[:, 64 * h : 64 * h + 64]
        absorbed[:, h, :, 512:] = jnp.concatenate([rope, rope], axis=1).reshape(16, BLK, 128)

    def decode_start():
        for h in range(16):
            dq[h, :, :512] = dot(step_nope[:, 128 * h : 128 * h + 128], ku[h])
            rope = step_rope[:, 64 * h : 64 * h + 64].astype(jnp.float32)
            dq[h, :, 512:] = jnp.concatenate([rope, rope], axis=1)
        q = dq[...].reshape(128, 640).astype(jnp.bfloat16)
        fresh = step_latent[...]
        s = dot_t(q[:, :576], fresh)
        row = lax.broadcasted_iota(jnp.int32, (128, 8), 0) % 8
        key = lax.broadcasted_iota(jnp.int32, (128, 8), 1)
        s = jnp.where((row // 2 == key // 2) & (key <= row), s, NEG)
        m = jnp.max(s, axis=1, keepdims=True)
        e = jnp.exp2((s - m) * EXP2)
        top[...] = jnp.broadcast_to(m, (128, 128))
        total[...] = jnp.broadcast_to(jnp.sum(e, axis=1, keepdims=True), (128, 128))
        acc[...] = dot(e.astype(jnp.bfloat16), fresh[:, :512])

    def decode(n):
        values, rope = keys_from(cache[n // 4, n % 4].reshape(16, 9, 16, 128))
        q = dq[...].reshape(128, 640).astype(jnp.bfloat16)
        s = dot_t(q, jnp.concatenate([values, rope], axis=1))
        row = lax.broadcasted_iota(jnp.int32, (128, 512), 0) % 8 // 2
        limit = jnp.where(row == 0, prefix[0], jnp.where(row == 1, prefix[1], jnp.where(row == 2, prefix[2], prefix[3])))
        place = lax.broadcasted_iota(jnp.int32, (128, 512), 1) + 512 * n
        s = jnp.where(place < limit, s, NEG)
        before = top[:, :1]
        m = jnp.maximum(before, jnp.max(s, axis=1, keepdims=True))
        keep = jnp.exp2((before - m) * EXP2)
        e = jnp.exp2((s - m) * EXP2)
        top[...] = jnp.broadcast_to(m, (128, 128))
        total[...] = total[...] * keep + jnp.sum(e, axis=1, keepdims=True)
        acc[...] = acc[...] * keep + dot(e.astype(jnp.bfloat16), values)

    step = 0
    for name in t.steps():
        if step == 0:
            for c in loads:
                c.wait()
        if step < 8:
            absorb(2 * step)
            absorb(2 * step + 1)
        elif step == 8:
            decode_start()
        step += 1
    own_copy.wait()
    for n in range(16):
        decode(n)
    decoded[...] = (acc[...] / total[:, :1]).reshape(16, 8, 512)


def attend_kernel(
    listed, slots, cache, absorbed, value_up, decoded,
    prefill_out, paged, decode_out,
    vu, ctx, out, paged_hold,
    s_in, s_out, s_paged,
):
    seq = lax.axis_index("seq")
    in_vu = pltpu.make_async_copy(value_up, vu, s_in)
    in_vu.start()

    def block(i):
        return cache[i // 64, i // 16 % 4, i // 4 % 4, i // 2 % 2, pl.ds(i % 2 * 9, 9)][None]

    def keys_of(n):
        here = seq * 16 + n
        blocks = [block(listed[n * VB + v]) for v in range(VB)]
        blocks += [block(jnp.maximum(here - SLASH + v, 0)) for v in range(SLASH + 1)]
        blocks.append(jnp.zeros((1, 9, 16, 128), jnp.bfloat16))
        return keys_from(jnp.concatenate(blocks, axis=0))

    col = lax.broadcasted_iota(jnp.int32, (BLK, 256), 1)
    row = lax.broadcasted_iota(jnp.int32, (BLK, 256), 0)
    causal = (col >= 128) & (col - 128 <= SLASH * BLK + row)

    def score(n):
        here = seq * 16 + n
        ok = causal & (here - SLASH + (col - 128) // BLK >= 0)
        for v in range(VB):
            ok = ok | ((col // BLK == v) & (listed[n * VB + v] <= here - SLASH - 1))
        bias = jnp.where(ok, 0.0, NEG)
        values, rope = keys_of(n)
        s = dot_t(absorbed[n].reshape(512, 640), jnp.concatenate([values, rope], axis=1))
        return (s.reshape(16, BLK, 256) + bias[None]).reshape(512, 256)

    def weigh(s):
        m = jnp.max(s, axis=1, keepdims=True)
        e = jnp.exp2((s - m) * EXP2)
        return e.astype(jnp.bfloat16), 1.0 / jnp.sum(e, axis=1, keepdims=True)

    def mix(n, e, inverse):
        got = dot(e, keys_of(n)[0]) * inverse
        start = pl.multiple_of(n * BLK, BLK)
        ctx[:, pl.ds(start, BLK), :] = got.astype(jnp.bfloat16).reshape(16, BLK, 512)

    shift = (
        lax.broadcasted_iota(jnp.int32, (128, 128), 0) == lax.broadcasted_iota(jnp.int32, (128, 128), 1) + 64
    ).astype(jnp.float32).astype(jnp.bfloat16)
    group = 3 * UNROLL

    def pages_out(k):
        ropes = []
        for j in range(group):
            i = k * group + j
            page = block(jnp.maximum(slots[i], 0))[0]
            page = jnp.where(slots[i] >= 0, page, jnp.zeros_like(page))
            for r in range(2):
                for w in range(4):
                    paged_hold[i, 16 * r : 16 * r + 16, 128 * w : 128 * w + 128] = page[4 * r + w]
            ropes.append(page[8])
        second = dot(jnp.concatenate(ropes, axis=0), shift).astype(jnp.bfloat16)
        for j in range(group):
            i = k * group + j
            paged_hold[i, :16, 512:576] = ropes[j][:, :64]
            paged_hold[i, 16:, 512:576] = second[16 * j : 16 * j + 16, :64]
        pages_copy(k).start()

    def pages_copy(k):
        part = pl.ds(k * group, group)
        return pltpu.make_async_copy(paged_hold.at[part], paged.at[0, part], s_paged.at[k])

    @pl.loop(0, 16 // UNROLL)
    def _(k):
        turns = [k * UNROLL + u for u in range(UNROLL)]
        scores = [score(n) for n in turns]
        weights = [weigh(s) for s in scores]
        for n, w in zip(turns, weights):
            mix(n, *w)
        pages_out(k)

    in_vu.wait()
    outs = []
    for h in range(16):
        cols = slice(128 * h, 128 * h + 128)
        out[:, cols] = dot(ctx[h], vu[h]).astype(jnp.bfloat16)
        got = dot(decoded[h].astype(jnp.bfloat16), vu[h]).astype(jnp.bfloat16)
        for b in range(4):
            decode_out[b, :, cols] = got[2 * b : 2 * b + 2]
        if h % 4 == 3:
            wide = slice(128 * (h - 3), 128 * h + 128)
            copy = pltpu.make_async_copy(out.at[:, wide], prefill_out.at[:, wide], s_out.at[h // 4])
            copy.start()
            outs.append(copy)
    for copy in outs:
        copy.wait()
    for k in range(16 // UNROLL):
        pages_copy(k).wait()


def gather_call(prefix_lengths, latent_cache, step_nope, step_rope, step_latent, query_nope, query_rope, key_up):
    vmem, smem, any_ = (pl.BlockSpec(memory_space=m) for m in (pltpu.VMEM, pltpu.SMEM, pl.ANY))
    bf16, f32 = jnp.bfloat16, jnp.float32
    dma = pltpu.SemaphoreType.DMA
    query_nope, query_rope, key_up = (
        pltpu.with_memory_space_constraint(x, pltpu.HBM) for x in (query_nope, query_rope, key_up)
    )
    return pl.pallas_call(
        gather_kernel,
        out_shape=(
            pltpu.VMEM((4, 4, 4, 2, 18, 16, 128), bf16),
            pltpu.VMEM((16, 16, BLK, 640), bf16),
            pltpu.VMEM((16, 8, 512), f32),
        ),
        in_specs=[smem, vmem, vmem, vmem, vmem, any_, any_, any_],
        out_specs=(vmem, vmem, vmem),
        scratch_shapes=[
            pltpu.VMEM((18, 16, 128), bf16),
            pltpu.VMEM((512, 2048), bf16),
            pltpu.VMEM((512, 1024), bf16),
            pltpu.VMEM((16, 128, 512), bf16),
            pltpu.VMEM((16, 8, 640), f32),
            pltpu.VMEM((128, 512), f32),
            pltpu.VMEM((128, 128), f32),
            pltpu.VMEM((128, 128), f32),
            dma((COPIES,)), dma((COPIES,)), dma((4,)),
        ],
        compiler_params=pltpu.CompilerParams(
            collective_id=0, has_side_effects=True, vmem_limit_bytes=16 << 20
        ),
        cost_estimate=pl.CostEstimate(flops=4 << 30, bytes_accessed=32 << 20, transcendentals=1 << 20),
        name="gather_absorb_decode",
    )(prefix_lengths, latent_cache, step_nope, step_rope, step_latent, query_nope, query_rope, key_up)


def attend_call(listed, slots, cache, absorbed, value_up, decoded):
    vmem, smem, any_ = (pl.BlockSpec(memory_space=m) for m in (pltpu.VMEM, pltpu.SMEM, pl.ANY))
    bf16 = jnp.bfloat16
    dma = pltpu.SemaphoreType.DMA
    cache, absorbed, decoded = (
        pltpu.with_memory_space_constraint(x, pltpu.VMEM) for x in (cache, absorbed, decoded)
    )
    value_up = pltpu.with_memory_space_constraint(value_up, pltpu.HBM)
    return pl.pallas_call(
        attend_kernel,
        out_shape=(
            jax.ShapeDtypeStruct((512, 2048), bf16),
            jax.ShapeDtypeStruct((1, 48, BLK, 576), bf16),
            jax.ShapeDtypeStruct((4, 2, 2048), bf16),
        ),
        in_specs=[smem, smem, vmem, vmem, any_, vmem],
        out_specs=(any_, any_, vmem),
        scratch_shapes=[
            pltpu.VMEM((16, 512, 128), bf16),
            pltpu.VMEM((16, 512, 512), bf16),
            pltpu.VMEM((512, 2048), bf16),
            pltpu.VMEM((48, BLK, 576), bf16),
            dma, dma((4,)), dma((4,)),
        ],
        compiler_params=pltpu.CompilerParams(vmem_limit_bytes=20 << 20),
        cost_estimate=pl.CostEstimate(flops=6 << 30, bytes_accessed=20 << 20, transcendentals=2 << 20),
        name="attend",
    )(listed, slots, cache, absorbed, value_up, decoded)


def on_device(
    query_nope, query_rope, latent_cache, key_up, value_up, vertical_lists, page_owner,
    step_nope, step_rope, step_latent, prefix_lengths,
):
    seq, dec = lax.axis_index("seq"), lax.axis_index("dec")
    cache, absorbed, decoded = gather_call(
        prefix_lengths, latent_cache, step_nope.reshape(8, 2048), step_rope.reshape(8, 1024),
        step_latent.reshape(8, 576), query_nope, query_rope, key_up,
    )
    listed = lax.dynamic_slice(vertical_lists, (dec, seq * 16, 0), (1, 16, VB)).reshape(64)
    owned = page_owner.reshape(16, 16) == dec
    rank = jnp.cumsum(owned.astype(jnp.int32), axis=1) - 1
    picks = owned[:, None, :] & (rank[:, None, :] == jnp.arange(3)[None, :, None])
    number = jnp.arange(256).reshape(16, 1, 16)
    slots = jnp.max(jnp.where(picks, number, -1), axis=2).reshape(48)
    return attend_call(listed, slots, cache, absorbed, value_up, decoded)


def solution(mesh):
    placed = (
        P("seq", "dec"), P("seq", "dec"), P(("seq", "dec"), None), P("dec", None, None), P("dec", None, None),
        P(), P(), P("seq", None, "dec"), P("seq", None, "dec"), P("seq", None, None), P("seq"),
    )
    return jax.shard_map(
        on_device,
        mesh=mesh,
        in_specs=placed,
        out_specs=(P("seq", "dec"), P("dec", None, None, None), P("seq", None, "dec")),
        check_vma=False,
    )
```

```python
import jax
import jax.numpy as jnp
from jax import lax
from jax.experimental import pallas as pl
from jax.experimental.pallas import tpu as pltpu
from jax.sharding import PartitionSpec as P

MESH = pl.DeviceIdType.MESH
ORDERS = (("x", "y", "z"), ("y", "z", "x"), ("z", "x", "y"))
ALL = slice(None)
COPIES = 200


class Gather:
    def __init__(self, cache, send, recv):
        seq, dec = lax.axis_index("seq"), lax.axis_index("dec")
        self.at = {"x": dec // 2, "y": seq // 4, "z": seq % 4}
        self.core = dec % 2
        self.cache, self.send, self.recv = cache, send, recv
        self.own = None
        self.sent, self.number, self.shares = [], {}, {}

    def device(self, axis=None, by=0, mate=False):
        at = dict(self.at)
        if axis is not None:
            at[axis] = (at[axis] + by + 4) % 4
        core = 1 - self.core if mate else self.core
        return (at["y"] * 4 + at["z"], at["x"] * 2 + core)

    def slot(self, mate=False):
        core = 1 - self.core if mate else self.core
        return self.cache.at[self.at["y"], self.at["z"], self.at["x"], core]

    def spot(self, axis, by):
        return (self.at[axis] + by + 4) % 4

    def chunk(self, g, rel, mate=False):
        where = []
        for axis in ("y", "z", "x"):
            r = rel[ORDERS[g].index(axis)]
            where.append(r if isinstance(r, slice) else (self.at[axis] + r + 4) % 4)
        core = 1 - self.core if mate else self.core
        return self.cache.at[where[0], where[1], where[2], core, pl.ds(6 * g, 6)]

    def copy(self, key, src, dst, target):
        k = self.number.setdefault(key, len(self.number))
        return pltpu.make_async_remote_copy(
            src_ref=src, dst_ref=dst, send_sem=self.send.at[k], recv_sem=self.recv.at[k],
            device_id=target, device_id_type=MESH)

    def hop(self, g, phase, rel, by):
        dst = self.chunk(g, rel)
        src = self.own.at[pl.ds(6 * g, 6)] if rel == (0, 0, 0) else dst
        key = (g, phase) + tuple(map(str, rel)) + (by,)
        copy = self.copy(key, src, dst, self.device(ORDERS[g][phase], by))
        copy.start()
        self.sent.append(copy)

    def land(self, g, phase, rel, by):
        got = list(rel)
        got[phase] = {0: -by, -by: 2}[rel[phase]]
        if got[phase] == -2:
            got[phase] = 2
        dst = self.chunk(g, got)
        key = (g, phase) + tuple(map(str, rel)) + (by,)
        self.copy(key, dst, dst, self.device(mate=True)).wait_recv()
        return tuple(got)

    def give(self, g, rel):
        src = self.chunk(g, rel)
        key = ("core", g) + tuple(map(str, rel))
        copy = self.copy(key, src, src, self.device(mate=True))
        copy.start()
        self.sent.append(copy)
        self.shares[key] = self.chunk(g, rel, mate=True)

    def give_own(self):
        copy = self.copy(("core",), self.own, self.slot(), self.device(mate=True))
        copy.start()
        self.sent.append(copy)
        self.shares[("core",)] = self.slot(mate=True)

    def wait_share(self, key):
        ref = self.shares.pop(key, None)
        if ref is not None:
            self.copy(key, ref, ref, self.device(mate=True)).wait_recv()

    def take(self, place):
        for g in range(3):
            rel = tuple(place[axis] for axis in ORDERS[g])
            if rel[1:] != (0, 0):
                rel = (ALL,) + rel[1:]
            self.wait_share(("core",) + (() if rel == (0, 0, 0) else (g,) + tuple(map(str, rel))))

    def finish(self):
        for key in list(self.shares):
            self.wait_share(key)
        for copy in self.sent:
            copy.wait_send()

    def barrier_start(self):
        sem = pltpu.get_barrier_semaphore()
        for axis in ("x", "y", "z"):
            for by in (-1, 1, 2):
                pl.semaphore_signal(sem, inc=1, device_id=self.device(axis, by), device_id_type=MESH)
        pl.semaphore_signal(sem, inc=1, device_id=self.device(mate=True), device_id_type=MESH)

    def barrier_wait(self):
        pl.semaphore_wait(pltpu.get_barrier_semaphore(), 10)

    def steps(self):
        three = range(3)
        near = (1, -1)
        for phase in (0, 1):
            for g in three:
                for by in near + (2,):
                    self.hop(g, phase, (0, 0, 0), by)
        for g in three:
            for by in near:
                self.hop(g, 2, (0, 0, 0), by)
        self.give_own()
        yield "own"
        for by in near + (2,):
            for g in three:
                got = self.land(g, 0, (0, 0, 0), by)
                for way in near + (2,):
                    self.hop(g, 1, got, way)
            yield "first"
        for by in near + (2,):
            for g in three:
                got = (-by if by != 2 else 2, 0, 0)
                for way in near:
                    self.hop(g, 2, got, way)
                self.give(g, got)
        yield "first"
        for by in near + (2,):
            for g in three:
                for r1 in (0, 1, -1, 2):
                    got = self.land(g, 1, (r1, 0, 0), by)
                got = (ALL,) + got[1:]
                for way in near:
                    self.hop(g, 2, got, way)
                self.give(g, got)
            yield "second"
        for g in three:
            for r1, on in ((0, 1), (1, -1), (-1, 1), (2, -1)):
                for by in near:
                    got = self.land(g, 2, (r1, 0, 0), by)
                    if by == on:
                        self.hop(g, 2, got, by)
            for r3 in near:
                self.give(g, (ALL, 0, r3))
            yield "third"
        yield (0, 1)
        for r2 in near + (2,):
            for g in three:
                for by in near:
                    got = self.land(g, 2, (ALL, r2, 0), by)
                    if r2 == 2:
                        self.hop(g, 2, (slice(0, 2) if by == 1 else slice(2, 4),) + got[1:], by)
                    elif r2 == by:
                        self.hop(g, 2, got, by)
                    self.give(g, got)
                yield "third"
            yield (r2, 1)
        for g in three:
            for r1, on in ((0, 1), (1, -1), (-1, 1), (2, -1)):
                self.land(g, 2, (r1, 0, -on), on)
            self.give(g, (ALL, 0, 2))
        yield (0, 2)
        for r2 in near:
            for g in three:
                self.give(g, self.land(g, 2, (ALL, r2, -r2), r2))
            yield (r2, 2)
        for g in three:
            self.land(g, 2, (slice(0, 2), 2, -1), 1)
            self.land(g, 2, (slice(2, 4), 2, 1), -1)
            self.give(g, (ALL, 2, 2))
        yield (2, 2)


MARKS = [(0, 1), (1, 1), (-1, 1), (2, 1), (0, 2), (1, 2), (-1, 2), (2, 2)]


def complete_at(place):
    last = 0
    for order in ORDERS:
        second, third = place[order[1]], place[order[2]]
        if third:
            last = max(last, MARKS.index((second, 2 if third == 2 else 1)))
    return last


BLK = 32
VB = 4
SLASH = 2
UNROLL = 4
QUANTA = 1
REL = (0, 1, -1, 2)
EXP2 = 192.0 ** -0.5 * 1.4426950408889634
NEG = float("-inf")


def dot(a, b):
    return jnp.dot(a, b, preferred_element_type=jnp.float32)


def dot_t(a, b):
    return lax.dot_general(a, b, (((1,), (1,)), ((), ())), preferred_element_type=jnp.float32)


def pack(rows, tiles):
    for b in range(2):
        for r in range(2):
            start = 32 * b + 16 * r
            for c in range(4):
                tiles[9 * b + 4 * r + c] = rows[start : start + 16, 128 * c : 128 * c + 128]
        tiles[9 * b + 8] = jnp.concatenate(
            [rows[32 * b : 32 * b + 16, 512:576], rows[32 * b + 16 : 32 * b + 32, 512:576]], axis=1
        )


def keys_from(blocks):
    n = blocks.shape[0]

    def rows(first, second):
        return jnp.stack([first, second], axis=1).reshape(n * BLK, 128)

    latent = jnp.concatenate([rows(blocks[:, w], blocks[:, 4 + w]) for w in range(4)], axis=1)
    tile = blocks[:, 8]
    low = lax.broadcasted_iota(jnp.int32, tile.shape, 2) < 64
    zero = jnp.zeros_like(tile)
    return latent, rows(jnp.where(low, tile, zero), jnp.where(low, zero, tile))


def gather_kernel(
    prefix_in, latent_in, lists_in, owner_in, nope_in, rope_in, fresh_in, query_nope, query_rope, key_up,
    cache, absorbed, decoded, listed, slots,
    prefix, latent, owner, step_nope, step_rope, step_latent, tiles, qn, qr, ku, sn, sl, dq, acc, top, total, slot_rows,
    send, recv, local,
):
    t = Gather(cache, send, recv)
    t.barrier_start()
    first = pltpu.make_async_copy(latent_in, latent, local.at[9])
    first.start()
    dec = lax.axis_index("dec")
    loads = [
        pltpu.make_async_copy(src, dst, local.at[i])
        for i, (src, dst) in enumerate(
            (
                (query_nope, qn), (key_up, ku), (query_rope, qr), (prefix_in, prefix), (lists_in.at[dec], listed),
                (owner_in, owner), (nope_in, step_nope), (rope_in, step_rope), (fresh_in, step_latent),
            )
        )
    ]
    for c in loads:
        c.start()
    first.wait()
    pack(latent, tiles)
    t.own = tiles
    t.barrier_wait()
    own_copy = pltpu.make_async_copy(tiles, t.slot(), local.at[10])
    own_copy.start()

    def page_slots():
        page = lax.broadcasted_iota(jnp.int32, (256, 256), 0)
        other = lax.broadcasted_iota(jnp.int32, (256, 256), 1)
        before = ((page // 16 == other // 16) & (page < other)).astype(jnp.float32).astype(jnp.bfloat16)
        owned = jnp.broadcast_to((owner[...] == dec).astype(jnp.float32), (8, 256))
        rank = dot(owned.astype(jnp.bfloat16), before)
        turn = lax.broadcasted_iota(jnp.int32, (8, 256), 0).astype(jnp.float32)
        pick = jnp.where((owned > 0) & (rank == turn), 1.0, 0.0)
        number = lax.broadcasted_iota(jnp.int32, (8, 256), 1).astype(jnp.float32)
        home = (
            lax.broadcasted_iota(jnp.int32, (256, 128), 0) // 16 == lax.broadcasted_iota(jnp.int32, (256, 128), 1)
        ).astype(jnp.float32).astype(jnp.bfloat16)
        which = dot((pick * number).astype(jnp.bfloat16), home)
        some = dot(pick.astype(jnp.bfloat16), home)
        slot_rows[...] = jnp.where(some > 0, which, -1.0).astype(jnp.int32)

    def absorb(h):
        got = dot(qn[:, 128 * h : 128 * h + 128], ku[h]).astype(jnp.bfloat16)
        absorbed[:, h, :, :512] = got.reshape(16, BLK, 512)
        rope = qr[:, 64 * h : 64 * h + 64]
        absorbed[:, h, :, 512:] = jnp.concatenate([rope, rope], axis=1).reshape(16, BLK, 128)

    def decode_start():
        for b in range(4):
            sn[2 * b : 2 * b + 2, :2048] = step_nope[b].astype(jnp.float32)
            sn[2 * b : 2 * b + 2, 2048:] = step_rope[b].astype(jnp.float32)
            sl[2 * b : 2 * b + 2] = step_latent[b].astype(jnp.float32)
        for h in range(16):
            dq[h, :, :512] = dot(sn[:, 128 * h : 128 * h + 128].astype(jnp.bfloat16), ku[h])
            rope = sn[:, 2048 + 64 * h : 2048 + 64 * h + 64]
            dq[h, :, 512:] = jnp.concatenate([rope, rope], axis=1)
        q = dq[...].reshape(128, 640).astype(jnp.bfloat16)
        fresh = sl[...].astype(jnp.bfloat16)
        s = dot_t(q[:, :576], fresh)
        row = lax.broadcasted_iota(jnp.int32, (128, 8), 0) % 8
        key = lax.broadcasted_iota(jnp.int32, (128, 8), 1)
        s = jnp.where((row // 2 == key // 2) & (key <= row), s, NEG)
        m = jnp.max(s, axis=1, keepdims=True)
        e = jnp.exp2((s - m) * EXP2)
        top[...] = jnp.broadcast_to(m, (128, 128))
        total[...] = jnp.broadcast_to(jnp.sum(e, axis=1, keepdims=True), (128, 128))
        acc[...] = dot(e.astype(jnp.bfloat16), fresh[:, :512])

    def decode(places):
        n = 128 * len(places)
        blocks, homes = [], []
        for place in places:
            t.take(place)
            y, z, x = (t.spot(axis, place[axis]) for axis in ("y", "z", "x"))
            blocks.append(cache[y, z, x].reshape(4, 9, 16, 128))
            homes.append(lax.broadcasted_iota(jnp.int32, (128, 128), 1) + 128 * (16 * y + 4 * z + x))
        values, rope = keys_from(jnp.concatenate(blocks, axis=0))
        q = dq[...].reshape(128, 640).astype(jnp.bfloat16)
        s = dot_t(q, jnp.concatenate([values, rope], axis=1))
        row = lax.broadcasted_iota(jnp.int32, (128, n), 0) % 8 // 2
        limit = jnp.where(row == 0, prefix[0], jnp.where(row == 1, prefix[1], jnp.where(row == 2, prefix[2], prefix[3])))
        place = jnp.concatenate(homes, axis=1)
        s = jnp.where(place < limit, s, NEG)
        before = top[:, :1]
        m = jnp.maximum(before, jnp.max(s, axis=1, keepdims=True))
        keep = jnp.exp2((before - m) * EXP2)
        e = jnp.exp2((s - m) * EXP2)
        top[...] = jnp.broadcast_to(m, (128, 128))
        total[...] = total[...] * keep + jnp.sum(e, axis=1, keepdims=True)
        acc[...] = acc[...] * keep + dot(e.astype(jnp.bfloat16), values)

    waiting = [dict(x=x, y=y, z=z) for x in REL for y in REL for z in REL]
    waiting.sort(key=complete_at)
    here = -1

    def decode_some(most, all_of=False):
        for _ in range(most):
            ready = [p for p in waiting if complete_at(p) <= here]
            if len(ready) >= 4 or (all_of and ready):
                decode(ready[:4])
                del waiting[: len(ready[:4])]

    step = 0
    for mark in t.steps():
        if step == 0:
            for c in loads:
                c.wait()
            page_slots()
            out_slots = pltpu.make_async_copy(slot_rows, slots, local.at[11])
            out_slots.start()
        if step < 8:
            absorb(2 * step)
            absorb(2 * step + 1)
        elif step == 8:
            decode_start()
            own_copy.wait()
        if mark in MARKS:
            here = MARKS.index(mark)
        if here >= 0:
            decode_some(QUANTA)
        step += 1
    decode_some(64, True)
    t.finish()
    out_slots.wait()
    decoded[...] = (acc[...] / total[:, :1]).reshape(16, 8, 512)


def attend_kernel(
    listed, slots, cache, absorbed, value_up, decoded,
    prefill_out, paged, decode_out,
    vu, ctx, out, paged_hold,
    s_in, s_out, s_paged,
):
    seq = lax.axis_index("seq")
    in_vu = pltpu.make_async_copy(value_up, vu, s_in)
    in_vu.start()

    def block(i):
        return cache[i // 64, i // 16 % 4, i // 4 % 4, i // 2 % 2, pl.ds(i % 2 * 9, 9)][None]

    def keys_of(n):
        here = seq * 16 + n
        blocks = [block(listed[v, here]) for v in range(VB)]
        blocks += [block(jnp.maximum(here - SLASH + v, 0)) for v in range(SLASH + 1)]
        blocks.append(jnp.zeros((1, 9, 16, 128), jnp.bfloat16))
        return keys_from(jnp.concatenate(blocks, axis=0))

    col = lax.broadcasted_iota(jnp.int32, (BLK, 256), 1)
    row = lax.broadcasted_iota(jnp.int32, (BLK, 256), 0)
    causal = (col >= 128) & (col - 128 <= SLASH * BLK + row)

    def score(n):
        here = seq * 16 + n
        ok = causal & (here - SLASH + (col - 128) // BLK >= 0)
        for v in range(VB):
            ok = ok | ((col // BLK == v) & (listed[v, here] <= here - SLASH - 1))
        bias = jnp.where(ok, 0.0, NEG)
        values, rope = keys_of(n)
        s = dot_t(absorbed[n].reshape(512, 640), jnp.concatenate([values, rope], axis=1))
        return (s.reshape(16, BLK, 256) + bias[None]).reshape(512, 256)

    def weigh(s):
        m = jnp.max(s, axis=1, keepdims=True)
        e = jnp.exp2((s - m) * EXP2)
        return e.astype(jnp.bfloat16), 1.0 / jnp.sum(e, axis=1, keepdims=True)

    def mix(n, e, inverse):
        got = dot(e, keys_of(n)[0]) * inverse
        start = pl.multiple_of(n * BLK, BLK)
        ctx[:, pl.ds(start, BLK), :] = got.astype(jnp.bfloat16).reshape(16, BLK, 512)

    shift = (
        lax.broadcasted_iota(jnp.int32, (128, 128), 0) == lax.broadcasted_iota(jnp.int32, (128, 128), 1) + 64
    ).astype(jnp.float32).astype(jnp.bfloat16)
    group = 3 * UNROLL

    def pages_out(k):
        ropes = []
        for j in range(group):
            i = k * group + j
            which = slots[j % 3, k * UNROLL + j // 3]
            page = block(jnp.maximum(which, 0))[0]
            page = jnp.where(which >= 0, page, jnp.zeros_like(page))
            for r in range(2):
                for w in range(4):
                    paged_hold[i, 16 * r : 16 * r + 16, 128 * w : 128 * w + 128] = page[4 * r + w]
            ropes.append(page[8])
        second = dot(jnp.concatenate(ropes, axis=0), shift).astype(jnp.bfloat16)
        for j in range(group):
            i = k * group + j
            paged_hold[i, :16, 512:576] = ropes[j][:, :64]
            paged_hold[i, 16:, 512:576] = second[16 * j : 16 * j + 16, :64]
        pages_copy(k).start()

    def pages_copy(k):
        part = pl.ds(k * group, group)
        return pltpu.make_async_copy(paged_hold.at[part], paged.at[0, part], s_paged.at[k])

    @pl.loop(0, 16 // UNROLL)
    def _(k):
        turns = [k * UNROLL + u for u in range(UNROLL)]
        scores = [score(n) for n in turns]
        weights = [weigh(s) for s in scores]
        for n, w in zip(turns, weights):
            mix(n, *w)
        pages_out(k)

    in_vu.wait()
    outs = []
    for h in range(16):
        cols = slice(128 * h, 128 * h + 128)
        out[:, cols] = dot(ctx[h], vu[h]).astype(jnp.bfloat16)
        got = dot(decoded[h].astype(jnp.bfloat16), vu[h]).astype(jnp.bfloat16)
        for b in range(4):
            decode_out[b, :, cols] = got[2 * b : 2 * b + 2]
        if h % 4 == 3:
            wide = slice(128 * (h - 3), 128 * h + 128)
            copy = pltpu.make_async_copy(out.at[:, wide], prefill_out.at[:, wide], s_out.at[h // 4])
            copy.start()
            outs.append(copy)
    for copy in outs:
        copy.wait()
    for k in range(16 // UNROLL):
        pages_copy(k).wait()


def gather_call(*args):
    vmem, any_ = pl.BlockSpec(memory_space=pltpu.VMEM), pl.BlockSpec(memory_space=pl.ANY)
    smem = pl.BlockSpec(memory_space=pltpu.SMEM)
    bf16, f32, i32 = jnp.bfloat16, jnp.float32, jnp.int32
    dma = pltpu.SemaphoreType.DMA
    args = [pltpu.with_memory_space_constraint(x, pltpu.HBM) for x in args]
    return pl.pallas_call(
        gather_kernel,
        out_shape=(
            pltpu.VMEM((4, 4, 4, 2, 18, 16, 128), bf16),
            pltpu.VMEM((16, 16, BLK, 640), bf16),
            pltpu.VMEM((16, 8, 512), f32),
            pltpu.SMEM((4, 256), i32),
            pltpu.SMEM((8, 128), i32),
        ),
        in_specs=[any_] * 10,
        out_specs=(vmem, vmem, vmem, smem, smem),
        scratch_shapes=[
            pltpu.SMEM((4,), i32),
            pltpu.VMEM((64, 576), bf16),
            pltpu.VMEM((1, 256), i32),
            pltpu.VMEM((4, 2, 2048), bf16),
            pltpu.VMEM((4, 2, 1024), bf16),
            pltpu.VMEM((4, 2, 576), bf16),
            pltpu.VMEM((18, 16, 128), bf16),
            pltpu.VMEM((512, 2048), bf16),
            pltpu.VMEM((512, 1024), bf16),
            pltpu.VMEM((16, 128, 512), bf16),
            pltpu.VMEM((8, 3072), f32),
            pltpu.VMEM((8, 576), f32),
            pltpu.VMEM((16, 8, 640), f32),
            pltpu.VMEM((128, 512), f32),
            pltpu.VMEM((128, 128), f32),
            pltpu.VMEM((128, 128), f32),
            pltpu.VMEM((8, 128), i32),
            dma((COPIES,)), dma((COPIES,)), dma((12,)),
        ],
        compiler_params=pltpu.CompilerParams(
            collective_id=0, has_side_effects=True, vmem_limit_bytes=16 << 20
        ),
        cost_estimate=pl.CostEstimate(flops=4 << 30, bytes_accessed=32 << 20, transcendentals=1 << 20),
        name="gather_absorb_decode",
    )(*args)


def attend_call(listed, slots, cache, absorbed, value_up, decoded):
    vmem, smem, any_ = (pl.BlockSpec(memory_space=m) for m in (pltpu.VMEM, pltpu.SMEM, pl.ANY))
    bf16 = jnp.bfloat16
    dma = pltpu.SemaphoreType.DMA
    cache, absorbed, decoded = (
        pltpu.with_memory_space_constraint(x, pltpu.VMEM) for x in (cache, absorbed, decoded)
    )
    listed, slots = (pltpu.with_memory_space_constraint(x, pltpu.SMEM) for x in (listed, slots))
    value_up = pltpu.with_memory_space_constraint(value_up, pltpu.HBM)
    return pl.pallas_call(
        attend_kernel,
        out_shape=(
            jax.ShapeDtypeStruct((512, 2048), bf16),
            jax.ShapeDtypeStruct((1, 48, BLK, 576), bf16),
            jax.ShapeDtypeStruct((4, 2, 2048), bf16),
        ),
        in_specs=[smem, smem, vmem, vmem, any_, vmem],
        out_specs=(any_, any_, vmem),
        scratch_shapes=[
            pltpu.VMEM((16, 512, 128), bf16),
            pltpu.VMEM((16, 512, 512), bf16),
            pltpu.VMEM((512, 2048), bf16),
            pltpu.VMEM((48, BLK, 576), bf16),
            dma, dma((4,)), dma((4,)),
        ],
        compiler_params=pltpu.CompilerParams(vmem_limit_bytes=20 << 20),
        cost_estimate=pl.CostEstimate(flops=6 << 30, bytes_accessed=20 << 20, transcendentals=2 << 20),
        name="attend",
    )(listed, slots, cache, absorbed, value_up, decoded)


def on_device(
    query_nope, query_rope, latent_cache, key_up, value_up, vertical_lists, page_owner,
    step_nope, step_rope, step_latent, prefix_lengths,
):
    cache, absorbed, decoded, listed, slots = gather_call(
        prefix_lengths, latent_cache, vertical_lists.transpose(0, 2, 1), page_owner.reshape(1, 256),
        step_nope, step_rope, step_latent, query_nope, query_rope, key_up,
    )
    return attend_call(listed, slots, cache, absorbed, value_up, decoded)


def solution(mesh):
    placed = (
        P("seq", "dec"), P("seq", "dec"), P(("seq", "dec"), None), P("dec", None, None), P("dec", None, None),
        P(), P(), P("seq", None, "dec"), P("seq", None, "dec"), P("seq", None, None), P("seq"),
    )
    return jax.shard_map(
        on_device,
        mesh=mesh,
        in_specs=placed,
        out_specs=(P("seq", "dec"), P("dec", None, None, None), P("seq", None, "dec")),
        check_vma=False,
    )
```

```python
import jax
import jax.numpy as jnp
from jax import lax
from jax.experimental import pallas as pl
from jax.experimental.pallas import tpu as pltpu
from jax.sharding import PartitionSpec as P

MESH = pl.DeviceIdType.MESH
ORDERS = (("x", "y", "z"), ("y", "z", "x"), ("z", "x", "y"))
ALL = slice(None)
COPIES = 200


class Gather:
    def __init__(self, cache, send, recv):
        seq, dec = lax.axis_index("seq"), lax.axis_index("dec")
        self.at = {"x": dec // 2, "y": seq // 4, "z": seq % 4}
        self.core = dec % 2
        self.cache, self.send, self.recv = cache, send, recv
        self.own = None
        self.sent, self.number, self.shares = [], {}, {}

    def device(self, axis=None, by=0, mate=False):
        at = dict(self.at)
        if axis is not None:
            at[axis] = (at[axis] + by + 4) % 4
        core = 1 - self.core if mate else self.core
        return (at["y"] * 4 + at["z"], at["x"] * 2 + core)

    def slot(self, mate=False):
        core = 1 - self.core if mate else self.core
        return self.cache.at[self.at["y"], self.at["z"], self.at["x"], core]

    def spot(self, axis, by):
        return (self.at[axis] + by + 4) % 4

    def chunk(self, g, rel, mate=False):
        where = []
        for axis in ("y", "z", "x"):
            r = rel[ORDERS[g].index(axis)]
            where.append(r if isinstance(r, slice) else (self.at[axis] + r + 4) % 4)
        core = 1 - self.core if mate else self.core
        return self.cache.at[where[0], where[1], where[2], core, pl.ds(6 * g, 6)]

    def copy(self, key, src, dst, target):
        k = self.number.setdefault(key, len(self.number))
        return pltpu.make_async_remote_copy(
            src_ref=src, dst_ref=dst, send_sem=self.send.at[k], recv_sem=self.recv.at[k],
            device_id=target, device_id_type=MESH)

    def hop(self, g, phase, rel, by):
        dst = self.chunk(g, rel)
        src = self.own.at[pl.ds(6 * g, 6)] if rel == (0, 0, 0) else dst
        key = (g, phase) + tuple(map(str, rel)) + (by,)
        copy = self.copy(key, src, dst, self.device(ORDERS[g][phase], by))
        copy.start()
        self.sent.append(copy)

    def land(self, g, phase, rel, by):
        got = list(rel)
        got[phase] = {0: -by, -by: 2}[rel[phase]]
        if got[phase] == -2:
            got[phase] = 2
        dst = self.chunk(g, got)
        key = (g, phase) + tuple(map(str, rel)) + (by,)
        self.copy(key, dst, dst, self.device(mate=True)).wait_recv()
        return tuple(got)

    def give(self, g, rel):
        src = self.chunk(g, rel)
        key = ("core", g) + tuple(map(str, rel))
        copy = self.copy(key, src, src, self.device(mate=True))
        copy.start()
        self.sent.append(copy)
        self.shares[key] = self.chunk(g, rel, mate=True)

    def give_own(self):
        copy = self.copy(("core",), self.own, self.slot(), self.device(mate=True))
        copy.start()
        self.sent.append(copy)
        self.shares[("core",)] = self.slot(mate=True)

    def wait_share(self, key):
        ref = self.shares.pop(key, None)
        if ref is not None:
            self.copy(key, ref, ref, self.device(mate=True)).wait_recv()

    def take(self, place):
        for g in range(3):
            rel = tuple(place[axis] for axis in ORDERS[g])
            if rel[1:] != (0, 0):
                rel = (ALL,) + rel[1:]
            self.wait_share(("core",) + (() if rel == (0, 0, 0) else (g,) + tuple(map(str, rel))))

    def finish(self):
        for key in list(self.shares):
            self.wait_share(key)
        for copy in self.sent:
            copy.wait_send()

    def barrier_start(self):
        sem = pltpu.get_barrier_semaphore()
        for axis in ("x", "y", "z"):
            for by in (-1, 1, 2):
                pl.semaphore_signal(sem, inc=1, device_id=self.device(axis, by), device_id_type=MESH)
        pl.semaphore_signal(sem, inc=1, device_id=self.device(mate=True), device_id_type=MESH)

    def barrier_wait(self):
        pl.semaphore_wait(pltpu.get_barrier_semaphore(), 10)

    def steps(self):
        three = range(3)
        near = (1, -1)
        for phase in (0, 1):
            for g in three:
                for by in near + (2,):
                    self.hop(g, phase, (0, 0, 0), by)
        for g in three:
            for by in near:
                self.hop(g, 2, (0, 0, 0), by)
        self.give_own()
        yield "own"
        for by in near + (2,):
            for g in three:
                got = self.land(g, 0, (0, 0, 0), by)
                for way in near + (2,):
                    self.hop(g, 1, got, way)
            yield "first"
        for by in near + (2,):
            for g in three:
                got = (-by if by != 2 else 2, 0, 0)
                for way in near:
                    self.hop(g, 2, got, way)
                self.give(g, got)
        yield "first"
        for by in near + (2,):
            for g in three:
                for r1 in (0, 1, -1, 2):
                    got = self.land(g, 1, (r1, 0, 0), by)
                got = (ALL,) + got[1:]
                for way in near:
                    self.hop(g, 2, got, way)
                self.give(g, got)
            yield "second"
        for g in three:
            for r1, on in ((0, 1), (1, -1), (-1, 1), (2, -1)):
                for by in near:
                    got = self.land(g, 2, (r1, 0, 0), by)
                    if by == on:
                        self.hop(g, 2, got, by)
            for r3 in near:
                self.give(g, (ALL, 0, r3))
            yield "third"
        yield (0, 1)
        for r2 in near + (2,):
            for g in three:
                for by in near:
                    got = self.land(g, 2, (ALL, r2, 0), by)
                    if r2 == 2:
                        self.hop(g, 2, (slice(0, 2) if by == 1 else slice(2, 4),) + got[1:], by)
                    elif r2 == by:
                        self.hop(g, 2, got, by)
                    self.give(g, got)
                yield "third"
            yield (r2, 1)
        for g in three:
            for r1, on in ((0, 1), (1, -1), (-1, 1), (2, -1)):
                self.land(g, 2, (r1, 0, -on), on)
            self.give(g, (ALL, 0, 2))
        yield (0, 2)
        for r2 in near:
            for g in three:
                self.give(g, self.land(g, 2, (ALL, r2, -r2), r2))
            yield (r2, 2)
        for g in three:
            self.land(g, 2, (slice(0, 2), 2, -1), 1)
            self.land(g, 2, (slice(2, 4), 2, 1), -1)
            self.give(g, (ALL, 2, 2))
        yield (2, 2)


MARKS = [(0, 1), (1, 1), (-1, 1), (2, 1), (0, 2), (1, 2), (-1, 2), (2, 2)]


def complete_at(place):
    last = 0
    for order in ORDERS:
        second, third = place[order[1]], place[order[2]]
        if third:
            last = max(last, MARKS.index((second, 2 if third == 2 else 1)))
    return last


BLK = 32
VB = 4
SLASH = 2
UNROLL = 4
EXP2 = 192.0 ** -0.5 * 1.4426950408889634
NEG = float("-inf")


def dot(a, b):
    return jnp.dot(a, b, preferred_element_type=jnp.float32)


def dot_t(a, b):
    return lax.dot_general(a, b, (((1,), (1,)), ((), ())), preferred_element_type=jnp.float32)


def pack(rows, tiles):
    for b in range(2):
        for r in range(2):
            start = 32 * b + 16 * r
            for c in range(4):
                tiles[9 * b + 4 * r + c] = rows[start : start + 16, 128 * c : 128 * c + 128]
        tiles[9 * b + 8] = jnp.concatenate(
            [rows[32 * b : 32 * b + 16, 512:576], rows[32 * b + 16 : 32 * b + 32, 512:576]], axis=1
        )


def keys_from(blocks):
    n = blocks.shape[0]

    def rows(first, second):
        return jnp.stack([first, second], axis=1).reshape(n * BLK, 128)

    latent = jnp.concatenate([rows(blocks[:, w], blocks[:, 4 + w]) for w in range(4)], axis=1)
    tile = blocks[:, 8]
    low = lax.broadcasted_iota(jnp.int32, tile.shape, 2) < 64
    zero = jnp.zeros_like(tile)
    return latent, rows(jnp.where(low, tile, zero), jnp.where(low, zero, tile))


def gather_kernel(
    prefix_in, latent_in, lists_in, owner_in, nope_in, rope_in, fresh_in, query_nope, query_rope, key_up,
    cache, absorbed, step_queries, acc, top, total, listed, slots, prefix,
    latent, owner, step_nope, step_rope, step_latent, tiles, qn, qr, ku, sn, sl, dq, slot_rows,
    send, recv, local,
):
    t = Gather(cache, send, recv)
    t.barrier_start()
    first = pltpu.make_async_copy(latent_in, latent, local.at[9])
    first.start()
    dec = lax.axis_index("dec")
    loads = [
        pltpu.make_async_copy(src, dst, local.at[i])
        for i, (src, dst) in enumerate(
            (
                (query_nope, qn), (key_up, ku), (query_rope, qr), (prefix_in, prefix), (lists_in.at[dec], listed),
                (owner_in, owner), (nope_in, step_nope), (rope_in, step_rope), (fresh_in, step_latent),
            )
        )
    ]
    for c in loads:
        c.start()
    first.wait()
    pack(latent, tiles)
    t.own = tiles
    t.barrier_wait()
    own_copy = pltpu.make_async_copy(tiles, t.slot(), local.at[10])
    own_copy.start()

    def page_slots():
        page = lax.broadcasted_iota(jnp.int32, (256, 256), 0)
        other = lax.broadcasted_iota(jnp.int32, (256, 256), 1)
        before = ((page // 16 == other // 16) & (page < other)).astype(jnp.float32).astype(jnp.bfloat16)
        owned = jnp.broadcast_to((owner[...] == dec).astype(jnp.float32), (8, 256))
        rank = dot(owned.astype(jnp.bfloat16), before)
        turn = lax.broadcasted_iota(jnp.int32, (8, 256), 0).astype(jnp.float32)
        pick = jnp.where((owned > 0) & (rank == turn), 1.0, 0.0)
        number = lax.broadcasted_iota(jnp.int32, (8, 256), 1).astype(jnp.float32)
        home = (
            lax.broadcasted_iota(jnp.int32, (256, 128), 0) // 16 == lax.broadcasted_iota(jnp.int32, (256, 128), 1)
        ).astype(jnp.float32).astype(jnp.bfloat16)
        which = dot((pick * number).astype(jnp.bfloat16), home)
        some = dot(pick.astype(jnp.bfloat16), home)
        slot_rows[...] = jnp.where(some > 0, which, -1.0).astype(jnp.int32)

    def absorb(h):
        got = dot(qn[:, 128 * h : 128 * h + 128], ku[h]).astype(jnp.bfloat16)
        absorbed[:, h, :, :512] = got.reshape(16, BLK, 512)
        rope = qr[:, 64 * h : 64 * h + 64]
        absorbed[:, h, :, 512:] = jnp.concatenate([rope, rope], axis=1).reshape(16, BLK, 128)

    def decode_start():
        for b in range(4):
            sn[2 * b : 2 * b + 2, :2048] = step_nope[b].astype(jnp.float32)
            sn[2 * b : 2 * b + 2, 2048:] = step_rope[b].astype(jnp.float32)
            sl[2 * b : 2 * b + 2] = step_latent[b].astype(jnp.float32)
        for h in range(16):
            dq[h, :, :512] = dot(sn[:, 128 * h : 128 * h + 128].astype(jnp.bfloat16), ku[h])
            rope = sn[:, 2048 + 64 * h : 2048 + 64 * h + 64]
            dq[h, :, 512:] = jnp.concatenate([rope, rope], axis=1)
        q = dq[...].reshape(128, 640).astype(jnp.bfloat16)
        step_queries[...] = q
        fresh = sl[...].astype(jnp.bfloat16)
        s = dot_t(q[:, :576], fresh)
        row = lax.broadcasted_iota(jnp.int32, (128, 8), 0) % 8
        key = lax.broadcasted_iota(jnp.int32, (128, 8), 1)
        s = jnp.where((row // 2 == key // 2) & (key <= row), s, NEG)
        m = jnp.max(s, axis=1, keepdims=True)
        e = jnp.exp2((s - m) * EXP2)
        top[...] = jnp.broadcast_to(m, (128, 128))
        total[...] = jnp.broadcast_to(jnp.sum(e, axis=1, keepdims=True), (128, 128))
        acc[...] = dot(e.astype(jnp.bfloat16), fresh[:, :512])

    for step, _ in enumerate(t.steps()):
        if step == 0:
            for c in loads:
                c.wait()
            page_slots()
            out_slots = pltpu.make_async_copy(slot_rows, slots, local.at[11])
            out_slots.start()
        if step < 8:
            absorb(2 * step)
            absorb(2 * step + 1)
        elif step == 8:
            decode_start()
    own_copy.wait()
    t.finish()
    out_slots.wait()


def attend_kernel(
    listed, slots, prefix, cache, absorbed, step_queries, acc_in, top_in, total_in, value_up,
    prefill_out, paged, decode_out,
    vu, ctx, out, paged_hold, acc, top, total, step_out,
    s_in, s_out, s_paged,
):
    seq = lax.axis_index("seq")
    in_vu = pltpu.make_async_copy(value_up, vu, s_in)
    in_vu.start()

    def block(i):
        return cache[i // 64, i // 16 % 4, i // 4 % 4, i // 2 % 2, pl.ds(i % 2 * 9, 9)][None]

    def keys_of(n):
        here = seq * 16 + n
        blocks = [block(listed[v, here]) for v in range(VB)]
        blocks += [block(jnp.maximum(here - SLASH + v, 0)) for v in range(SLASH + 1)]
        blocks.append(jnp.zeros((1, 9, 16, 128), jnp.bfloat16))
        return keys_from(jnp.concatenate(blocks, axis=0))

    col = lax.broadcasted_iota(jnp.int32, (BLK, 256), 1)
    row = lax.broadcasted_iota(jnp.int32, (BLK, 256), 0)
    causal = (col >= 128) & (col - 128 <= SLASH * BLK + row)

    def score(n):
        here = seq * 16 + n
        ok = causal & (here - SLASH + (col - 128) // BLK >= 0)
        for v in range(VB):
            ok = ok | ((col // BLK == v) & (listed[v, here] <= here - SLASH - 1))
        bias = jnp.where(ok, 0.0, NEG)
        values, rope = keys_of(n)
        s = dot_t(absorbed[n].reshape(512, 640), jnp.concatenate([values, rope], axis=1))
        return (s.reshape(16, BLK, 256) + bias[None]).reshape(512, 256)

    def weigh(s):
        m = jnp.max(s, axis=1, keepdims=True)
        e = jnp.exp2((s - m) * EXP2)
        return e.astype(jnp.bfloat16), 1.0 / jnp.sum(e, axis=1, keepdims=True)

    def mix(n, e, inverse):
        got = dot(e, keys_of(n)[0]) * inverse
        start = pl.multiple_of(n * BLK, BLK)
        ctx[:, pl.ds(start, BLK), :] = got.astype(jnp.bfloat16).reshape(16, BLK, 512)

    shift = (
        lax.broadcasted_iota(jnp.int32, (128, 128), 0) == lax.broadcasted_iota(jnp.int32, (128, 128), 1) + 64
    ).astype(jnp.float32).astype(jnp.bfloat16)
    group = 3 * UNROLL

    def pages_out(k):
        ropes = []
        for j in range(group):
            i = k * group + j
            which = slots[j % 3, k * UNROLL + j // 3]
            page = block(jnp.maximum(which, 0))[0]
            page = jnp.where(which >= 0, page, jnp.zeros_like(page))
            for r in range(2):
                for w in range(4):
                    paged_hold[i, 16 * r : 16 * r + 16, 128 * w : 128 * w + 128] = page[4 * r + w]
            ropes.append(page[8])
        second = dot(jnp.concatenate(ropes, axis=0), shift).astype(jnp.bfloat16)
        for j in range(group):
            i = k * group + j
            paged_hold[i, :16, 512:576] = ropes[j][:, :64]
            paged_hold[i, 16:, 512:576] = second[16 * j : 16 * j + 16, :64]
        pages_copy(k).start()

    def pages_copy(k):
        part = pl.ds(k * group, group)
        return pltpu.make_async_copy(paged_hold.at[part], paged.at[0, part], s_paged.at[k])

    acc[...] = acc_in[...]
    top[...] = top_in[...]
    total[...] = total_in[...]
    step_row = lax.broadcasted_iota(jnp.int32, (128, 128), 0) % 8 // 2
    limit = jnp.where(step_row == 3, prefix[3], prefix[0])
    for b in (1, 2):
        limit = jnp.where(step_row == b, prefix[b], limit)

    def decode_score(y):
        values, rope = keys_from(cache[y].reshape(64, 9, 16, 128))
        s = dot_t(step_queries[...], jnp.concatenate([values, rope], axis=1))
        place = lax.broadcasted_iota(jnp.int32, (128, 2048), 1) + 2048 * y
        return jnp.where(place < limit[:, :1], s, NEG)

    def decode_weigh(s):
        before = top[...]
        m = jnp.maximum(before, jnp.max(s, axis=1, keepdims=True))
        keep = jnp.exp2((before - m) * EXP2)
        e = jnp.exp2((s - m[:, :1]) * EXP2)
        top[...] = m
        total[...] = total[...] * keep + jnp.sum(e, axis=1, keepdims=True)
        return e.astype(jnp.bfloat16), keep[:, :1]

    def decode_mix(y, e, keep):
        values = keys_from(cache[y].reshape(64, 9, 16, 128))[0]
        acc[...] = acc[...] * keep + dot(e, values)

    @pl.loop(0, 16 // UNROLL)
    def _(k):
        turns = [k * UNROLL + u for u in range(UNROLL)]
        scores = [score(n) for n in turns]
        ds = decode_score(k)
        weights = [weigh(s) for s in scores]
        dw = decode_weigh(ds)
        for n, w in zip(turns, weights):
            mix(n, *w)
        decode_mix(k, *dw)
        pages_out(k)

    in_vu.wait()
    decoded = (acc[...] / total[:, :1]).reshape(16, 8, 512).astype(jnp.bfloat16)
    outs = []
    for h in range(16):
        cols = slice(128 * h, 128 * h + 128)
        got = dot(decoded[h], vu[h]).astype(jnp.bfloat16)
        for b in range(4):
            step_out[b, :, cols] = got[2 * b : 2 * b + 2]
        out[:, cols] = dot(ctx[h], vu[h]).astype(jnp.bfloat16)
        if h % 2 == 1:
            wide = slice(128 * (h - 1), 128 * h + 128)
            outs.append(pltpu.make_async_copy(out.at[:, wide], prefill_out.at[:, wide], s_out.at[h // 2]))
            outs[-1].start()
    outs.append(pltpu.make_async_copy(step_out, decode_out, s_out.at[8]))
    outs[-1].start()
    for copy in outs:
        copy.wait()
    for k in range(16 // UNROLL):
        pages_copy(k).wait()


def gather_call(*args):
    vmem, any_ = pl.BlockSpec(memory_space=pltpu.VMEM), pl.BlockSpec(memory_space=pl.ANY)
    smem = pl.BlockSpec(memory_space=pltpu.SMEM)
    bf16, f32, i32 = jnp.bfloat16, jnp.float32, jnp.int32
    dma = pltpu.SemaphoreType.DMA
    args = [pltpu.with_memory_space_constraint(x, pltpu.HBM) for x in args]
    return pl.pallas_call(
        gather_kernel,
        out_shape=(
            pltpu.VMEM((4, 4, 4, 2, 18, 16, 128), bf16),
            pltpu.VMEM((16, 16, BLK, 640), bf16),
            pltpu.VMEM((128, 640), bf16),
            pltpu.VMEM((128, 512), f32),
            pltpu.VMEM((128, 128), f32),
            pltpu.VMEM((128, 128), f32),
            pltpu.SMEM((4, 256), i32),
            pltpu.SMEM((8, 128), i32),
            pltpu.SMEM((4,), i32),
        ),
        in_specs=[any_] * 10,
        out_specs=(vmem,) * 6 + (smem,) * 3,
        scratch_shapes=[
            pltpu.VMEM((64, 576), bf16),
            pltpu.VMEM((1, 256), i32),
            pltpu.VMEM((4, 2, 2048), bf16),
            pltpu.VMEM((4, 2, 1024), bf16),
            pltpu.VMEM((4, 2, 576), bf16),
            pltpu.VMEM((18, 16, 128), bf16),
            pltpu.VMEM((512, 2048), bf16),
            pltpu.VMEM((512, 1024), bf16),
            pltpu.VMEM((16, 128, 512), bf16),
            pltpu.VMEM((8, 3072), f32),
            pltpu.VMEM((8, 576), f32),
            pltpu.VMEM((16, 8, 640), f32),
            pltpu.VMEM((8, 128), i32),
            dma((COPIES,)), dma((COPIES,)), dma((12,)),
        ],
        compiler_params=pltpu.CompilerParams(
            collective_id=0, has_side_effects=True, vmem_limit_bytes=16 << 20
        ),
        cost_estimate=pl.CostEstimate(flops=4 << 30, bytes_accessed=32 << 20, transcendentals=1 << 20),
        name="gather_absorb_decode",
    )(*args)


def attend_call(cache, absorbed, step_queries, acc, top, total, listed, slots, prefix, value_up):
    vmem, smem, any_ = (pl.BlockSpec(memory_space=m) for m in (pltpu.VMEM, pltpu.SMEM, pl.ANY))
    bf16, f32 = jnp.bfloat16, jnp.float32
    dma = pltpu.SemaphoreType.DMA
    large = [pltpu.with_memory_space_constraint(x, pltpu.VMEM) for x in (cache, absorbed, step_queries, acc, top, total)]
    small = [pltpu.with_memory_space_constraint(x, pltpu.SMEM) for x in (listed, slots, prefix)]
    value_up = pltpu.with_memory_space_constraint(value_up, pltpu.HBM)
    return pl.pallas_call(
        attend_kernel,
        out_shape=(
            jax.ShapeDtypeStruct((512, 2048), bf16),
            jax.ShapeDtypeStruct((1, 48, BLK, 576), bf16),
            jax.ShapeDtypeStruct((4, 2, 2048), bf16),
        ),
        in_specs=[smem] * 3 + [vmem] * 6 + [any_],
        out_specs=(any_, any_, any_),
        scratch_shapes=[
            pltpu.VMEM((16, 512, 128), bf16),
            pltpu.VMEM((16, 512, 512), bf16),
            pltpu.VMEM((512, 2048), bf16),
            pltpu.VMEM((48, BLK, 576), bf16),
            pltpu.VMEM((128, 512), f32),
            pltpu.VMEM((128, 128), f32),
            pltpu.VMEM((128, 128), f32),
            pltpu.VMEM((4, 2, 2048), bf16),
            dma, dma((9,)), dma((4,)),
        ],
        compiler_params=pltpu.CompilerParams(vmem_limit_bytes=34 << 20),
        cost_estimate=pl.CostEstimate(flops=8 << 30, bytes_accessed=20 << 20, transcendentals=3 << 20),
        name="attend",
    )(*small, *large, value_up)


def on_device(
    query_nope, query_rope, latent_cache, key_up, value_up, vertical_lists, page_owner,
    step_nope, step_rope, step_latent, prefix_lengths,
):
    kept = gather_call(
        prefix_lengths, latent_cache, vertical_lists.transpose(0, 2, 1), page_owner.reshape(1, 256),
        step_nope, step_rope, step_latent, query_nope, query_rope, key_up,
    )
    return attend_call(*kept, value_up)


def solution(mesh):
    placed = (
        P("seq", "dec"), P("seq", "dec"), P(("seq", "dec"), None), P("dec", None, None), P("dec", None, None),
        P(), P(), P("seq", None, "dec"), P("seq", None, "dec"), P("seq", None, None), P("seq"),
    )
    return jax.shard_map(
        on_device,
        mesh=mesh,
        in_specs=placed,
        out_specs=(P("seq", "dec"), P("dec", None, None, None), P("seq", None, "dec")),
        check_vma=False,
    )
```

```python
import jax
import jax.numpy as jnp
from jax import lax
from jax.experimental import pallas as pl
from jax.experimental.pallas import tpu as pltpu
from jax.sharding import PartitionSpec as P

MESH = pl.DeviceIdType.MESH
ORDERS = (("x", "y", "z"), ("y", "z", "x"), ("z", "x", "y"))
ALL = slice(None)
COPIES = 200


class Gather:
    def __init__(self, cache, send, recv):
        seq, dec = lax.axis_index("seq"), lax.axis_index("dec")
        self.at = {"x": dec // 2, "y": seq // 4, "z": seq % 4}
        self.core = dec % 2
        self.cache, self.send, self.recv = cache, send, recv
        self.own = None
        self.sent, self.number, self.shares = [], {}, {}

    def device(self, axis=None, by=0, mate=False):
        at = dict(self.at)
        if axis is not None:
            at[axis] = (at[axis] + by + 4) % 4
        core = 1 - self.core if mate else self.core
        return (at["y"] * 4 + at["z"], at["x"] * 2 + core)

    def slot(self, mate=False):
        core = 1 - self.core if mate else self.core
        return self.cache.at[self.at["y"], self.at["z"], self.at["x"], core]

    def spot(self, axis, by):
        return (self.at[axis] + by + 4) % 4

    def chunk(self, g, rel, mate=False):
        where = []
        for axis in ("y", "z", "x"):
            r = rel[ORDERS[g].index(axis)]
            where.append(r if isinstance(r, slice) else (self.at[axis] + r + 4) % 4)
        core = 1 - self.core if mate else self.core
        return self.cache.at[where[0], where[1], where[2], core, pl.ds(6 * g, 6)]

    def copy(self, key, src, dst, target):
        k = self.number.setdefault(key, len(self.number))
        return pltpu.make_async_remote_copy(
            src_ref=src, dst_ref=dst, send_sem=self.send.at[k], recv_sem=self.recv.at[k],
            device_id=target, device_id_type=MESH)

    def hop(self, g, phase, rel, by):
        dst = self.chunk(g, rel)
        src = self.own.at[pl.ds(6 * g, 6)] if rel == (0, 0, 0) else dst
        key = (g, phase) + tuple(map(str, rel)) + (by,)
        copy = self.copy(key, src, dst, self.device(ORDERS[g][phase], by))
        copy.start()
        self.sent.append(copy)

    def land(self, g, phase, rel, by):
        got = list(rel)
        got[phase] = {0: -by, -by: 2}[rel[phase]]
        if got[phase] == -2:
            got[phase] = 2
        dst = self.chunk(g, got)
        key = (g, phase) + tuple(map(str, rel)) + (by,)
        self.copy(key, dst, dst, self.device(mate=True)).wait_recv()
        return tuple(got)

    def give(self, g, rel):
        src = self.chunk(g, rel)
        key = ("core", g) + tuple(map(str, rel))
        copy = self.copy(key, src, src, self.device(mate=True))
        copy.start()
        self.sent.append(copy)
        self.shares[key] = self.chunk(g, rel, mate=True)

    def give_own(self):
        copy = self.copy(("core",), self.own, self.slot(), self.device(mate=True))
        copy.start()
        self.sent.append(copy)
        self.shares[("core",)] = self.slot(mate=True)

    def wait_share(self, key):
        ref = self.shares.pop(key, None)
        if ref is not None:
            self.copy(key, ref, ref, self.device(mate=True)).wait_recv()

    def take(self, place):
        for g in range(3):
            rel = tuple(place[axis] for axis in ORDERS[g])
            if rel[1:] != (0, 0):
                rel = (ALL,) + rel[1:]
            self.wait_share(("core",) + (() if rel == (0, 0, 0) else (g,) + tuple(map(str, rel))))

    def finish(self):
        for key in list(self.shares):
            self.wait_share(key)
        for copy in self.sent:
            copy.wait_send()

    def barrier_start(self):
        sem = pltpu.get_barrier_semaphore()
        for axis in ("x", "y", "z"):
            for by in (-1, 1, 2):
                pl.semaphore_signal(sem, inc=1, device_id=self.device(axis, by), device_id_type=MESH)
        pl.semaphore_signal(sem, inc=1, device_id=self.device(mate=True), device_id_type=MESH)

    def barrier_wait(self):
        pl.semaphore_wait(pltpu.get_barrier_semaphore(), 10)

    def steps(self):
        three = range(3)
        near = (1, -1)
        for phase in (0, 1):
            for g in three:
                for by in near + (2,):
                    self.hop(g, phase, (0, 0, 0), by)
        for g in three:
            for by in near:
                self.hop(g, 2, (0, 0, 0), by)
        self.give_own()
        yield "own"
        for by in near + (2,):
            for g in three:
                got = self.land(g, 0, (0, 0, 0), by)
                for way in near + (2,):
                    self.hop(g, 1, got, way)
            yield "first"
        for by in near + (2,):
            for g in three:
                got = (-by if by != 2 else 2, 0, 0)
                for way in near:
                    self.hop(g, 2, got, way)
                self.give(g, got)
        yield "first"
        for by in near + (2,):
            for g in three:
                for r1 in (0, 1, -1, 2):
                    got = self.land(g, 1, (r1, 0, 0), by)
                got = (ALL,) + got[1:]
                for way in near:
                    self.hop(g, 2, got, way)
                self.give(g, got)
            yield "second"
        for g in three:
            for r1, on in ((0, 1), (1, -1), (-1, 1), (2, -1)):
                for by in near:
                    got = self.land(g, 2, (r1, 0, 0), by)
                    if by == on:
                        self.hop(g, 2, got, by)
            for r3 in near:
                self.give(g, (ALL, 0, r3))
            yield "third"
        yield (0, 1)
        for r2 in near + (2,):
            for g in three:
                for by in near:
                    got = self.land(g, 2, (ALL, r2, 0), by)
                    if r2 == 2:
                        self.hop(g, 2, (slice(0, 2) if by == 1 else slice(2, 4),) + got[1:], by)
                    elif r2 == by:
                        self.hop(g, 2, got, by)
                    self.give(g, got)
                yield "third"
            yield (r2, 1)
        for g in three:
            for r1, on in ((0, 1), (1, -1), (-1, 1), (2, -1)):
                self.land(g, 2, (r1, 0, -on), on)
            self.give(g, (ALL, 0, 2))
        yield (0, 2)
        for r2 in near:
            for g in three:
                self.give(g, self.land(g, 2, (ALL, r2, -r2), r2))
            yield (r2, 2)
        for g in three:
            self.land(g, 2, (slice(0, 2), 2, -1), 1)
            self.land(g, 2, (slice(2, 4), 2, 1), -1)
            self.give(g, (ALL, 2, 2))
        yield (2, 2)


MARKS = [(0, 1), (1, 1), (-1, 1), (2, 1), (0, 2), (1, 2), (-1, 2), (2, 2)]


def complete_at(place):
    last = 0
    for order in ORDERS:
        second, third = place[order[1]], place[order[2]]
        if third:
            last = max(last, MARKS.index((second, 2 if third == 2 else 1)))
    return last


BLK = 32
VB = 4
SLASH = 2
UNROLL = 4
EXP2 = 192.0 ** -0.5 * 1.4426950408889634
NEG = float("-inf")
LEAST = -3.0e38
REL = (0, 1, -1, 2)
PLAN = {(2, 1): 24, (-1, 2): 24}


def dot(a, b):
    return jnp.dot(a, b, preferred_element_type=jnp.float32)


def dot_t(a, b):
    return lax.dot_general(a, b, (((1,), (1,)), ((), ())), preferred_element_type=jnp.float32)


def pack(rows, tiles):
    for b in range(2):
        for r in range(2):
            start = 32 * b + 16 * r
            for c in range(4):
                tiles[9 * b + 4 * r + c] = rows[start : start + 16, 128 * c : 128 * c + 128]
        tiles[9 * b + 8] = jnp.concatenate(
            [rows[32 * b : 32 * b + 16, 512:576], rows[32 * b + 16 : 32 * b + 32, 512:576]], axis=1
        )


def keys_from(blocks):
    n = blocks.shape[0]

    def rows(first, second):
        return jnp.stack([first, second], axis=1).reshape(n * BLK, 128)

    latent = jnp.concatenate([rows(blocks[:, w], blocks[:, 4 + w]) for w in range(4)], axis=1)
    tile = blocks[:, 8]
    low = lax.broadcasted_iota(jnp.int32, tile.shape, 2) < 64
    zero = jnp.zeros_like(tile)
    return latent, rows(jnp.where(low, tile, zero), jnp.where(low, zero, tile))


def gather_kernel(
    prefix_in, latent_in, lists_in, owner_in, nope_in, rope_in, fresh_in, query_nope, query_rope, key_up,
    cache, absorbed, mine, theirs, listed, slots, prefix,
    latent, owner, step_nope, step_rope, step_latent, tiles, qn, qr, ku, sn, sl, dq, queries, gone, acc, top, total, slot_rows,
    send, recv, local,
):
    t = Gather(cache, send, recv)
    t.barrier_start()
    first = pltpu.make_async_copy(latent_in, latent, local.at[9])
    first.start()
    dec = lax.axis_index("dec")
    loads = [
        pltpu.make_async_copy(src, dst, local.at[i])
        for i, (src, dst) in enumerate(
            (
                (query_nope, qn), (key_up, ku), (query_rope, qr), (prefix_in, prefix), (lists_in.at[dec], listed),
                (owner_in, owner), (nope_in, step_nope), (rope_in, step_rope), (fresh_in, step_latent),
            )
        )
    ]
    for c in loads:
        c.start()
    first.wait()
    pack(latent, tiles)
    t.own = tiles
    t.barrier_wait()
    own_copy = pltpu.make_async_copy(tiles, t.slot(), local.at[10])
    own_copy.start()

    def page_slots():
        page = lax.broadcasted_iota(jnp.int32, (256, 256), 0)
        other = lax.broadcasted_iota(jnp.int32, (256, 256), 1)
        before = ((page // 16 == other // 16) & (page < other)).astype(jnp.float32).astype(jnp.bfloat16)
        owned = jnp.broadcast_to((owner[...] == dec).astype(jnp.float32), (8, 256))
        rank = dot(owned.astype(jnp.bfloat16), before)
        turn = lax.broadcasted_iota(jnp.int32, (8, 256), 0).astype(jnp.float32)
        pick = jnp.where((owned > 0) & (rank == turn), 1.0, 0.0)
        number = lax.broadcasted_iota(jnp.int32, (8, 256), 1).astype(jnp.float32)
        home = (
            lax.broadcasted_iota(jnp.int32, (256, 128), 0) // 16 == lax.broadcasted_iota(jnp.int32, (256, 128), 1)
        ).astype(jnp.float32).astype(jnp.bfloat16)
        which = dot((pick * number).astype(jnp.bfloat16), home)
        some = dot(pick.astype(jnp.bfloat16), home)
        slot_rows[...] = jnp.where(some > 0, which, -1.0).astype(jnp.int32)

    def absorb(h):
        got = dot(qn[:, 128 * h : 128 * h + 128], ku[h]).astype(jnp.bfloat16)
        absorbed[:, h, :, :512] = got.reshape(16, BLK, 512)
        rope = qr[:, 64 * h : 64 * h + 64]
        absorbed[:, h, :, 512:] = jnp.concatenate([rope, rope], axis=1).reshape(16, BLK, 128)

    def decode_start():
        for b in range(4):
            sn[2 * b : 2 * b + 2, :2048] = step_nope[b].astype(jnp.float32)
            sn[2 * b : 2 * b + 2, 2048:] = step_rope[b].astype(jnp.float32)
            sl[2 * b : 2 * b + 2] = step_latent[b].astype(jnp.float32)
        for h in range(16):
            dq[h, :, :512] = dot(sn[:, 128 * h : 128 * h + 128].astype(jnp.bfloat16), ku[h])
            rope = sn[:, 2048 + 64 * h : 2048 + 64 * h + 64]
            dq[h, :, 512:] = jnp.concatenate([rope, rope], axis=1)
        queries[0] = dq[...].reshape(128, 640).astype(jnp.bfloat16)
        ask.start()

    def decode_fresh():
        fresh = sl[...].astype(jnp.bfloat16)
        s = dot_t(queries[0, :, :576], fresh)
        row = lax.broadcasted_iota(jnp.int32, (128, 8), 0) % 8
        key = lax.broadcasted_iota(jnp.int32, (128, 8), 1)
        s = jnp.where((row // 2 == key // 2) & (key <= row), s, NEG)
        m = jnp.max(s, axis=1, keepdims=True)
        e = jnp.exp2((s - m) * EXP2)
        top[:128] = jnp.broadcast_to(m, (128, 128))
        total[:128] = jnp.broadcast_to(jnp.sum(e, axis=1, keepdims=True), (128, 128))
        acc[:128] = dot(e.astype(jnp.bfloat16), fresh[:, :512])
        top[128:] = jnp.full((128, 128), LEAST)
        total[128:] = jnp.zeros((128, 128), jnp.float32)
        acc[128:] = jnp.zeros((128, 512), jnp.float32)

    def decode(places):
        blocks, homes = [], []
        half = lax.broadcasted_iota(jnp.int32, (1, 128), 1)
        for i, place in enumerate(places):
            y, z, x = (t.spot(axis, place[axis]) for axis in ("y", "z", "x"))
            blocks.append(cache[y, z, x, t.core].reshape(2, 9, 16, 128))
            homes.append(512 * (4 * y + z) + 128 * x + 64 * t.core)
        place = jnp.concatenate(
            [jnp.where(half < 64, homes[i] + half, homes[i + 1] + half - 64) for i in range(0, len(homes), 2)], axis=1
        )
        values, rope = keys_from(jnp.concatenate(blocks, axis=0))
        q = queries[...].reshape(256, 640)
        s = dot_t(q, jnp.concatenate([values, rope], axis=1))
        row = lax.broadcasted_iota(jnp.int32, (256, 1), 0) % 8 // 2
        limit = jnp.where(row == 3, prefix[3], prefix[0])
        for b in (1, 2):
            limit = jnp.where(row == b, prefix[b], limit)
        s = jnp.where(place < limit, s, NEG)
        before = top[...]
        m = jnp.maximum(before, jnp.max(s, axis=1, keepdims=True))
        keep = jnp.exp2((before - m) * EXP2)
        e = jnp.exp2((s - m[:, :1]) * EXP2)
        top[...] = m
        total[...] = total[...] * keep + jnp.sum(e, axis=1, keepdims=True)
        acc[...] = acc[...] * keep[:, :1] + dot(e.astype(jnp.bfloat16), values)

    def mate_copy(k, src, dst):
        return pltpu.make_async_remote_copy(
            src_ref=src, dst_ref=dst, send_sem=send.at[COPIES + k], recv_sem=recv.at[COPIES + k],
            device_id=t.device(mate=True), device_id_type=MESH)

    ask = mate_copy(0, queries.at[0], queries.at[1])
    answer = mate_copy(1, gone, theirs)

    waiting = [dict(x=x, y=y, z=z) for x in REL for y in REL for z in REL]
    waiting.sort(key=complete_at)

    def decode_next(size):
        decode(waiting[:size])
        del waiting[:size]

    for step, mark in enumerate(t.steps()):
        if step == 0:
            for c in loads:
                c.wait()
            page_slots()
            out_slots = pltpu.make_async_copy(slot_rows, slots, local.at[11])
            out_slots.start()
        if step < 8:
            absorb(2 * step)
            absorb(2 * step + 1)
        elif step == 8:
            decode_start()
        elif step == 9:
            decode_fresh()
            own_copy.wait()
            ask.wait()
        size = PLAN.get(mark, 0)
        if size:
            assert all(MARKS.index(mark) >= complete_at(p) for p in waiting[:size])
            decode_next(size)
    while waiting:
        decode_next(min(len(waiting), 16))
    gone[:, :512] = acc[128:]
    gone[:, 512:640] = top[128:]
    gone[:, 640:] = total[128:]
    answer.start()
    mine[:, :512] = acc[:128]
    mine[:, 512:640] = top[:128]
    mine[:, 640:] = total[:128]
    t.finish()
    out_slots.wait()
    answer.wait()


def attend_kernel(
    listed, slots, cache, absorbed, mine, theirs, value_up,
    prefill_out, paged, decode_out,
    vu, ctx, out, paged_hold, step_out,
    s_in, s_out, s_paged,
):
    seq = lax.axis_index("seq")
    in_vu = pltpu.make_async_copy(value_up, vu, s_in)
    in_vu.start()

    def block(i):
        return cache[i // 64, i // 16 % 4, i // 4 % 4, i // 2 % 2, pl.ds(i % 2 * 9, 9)][None]

    def keys_of(n):
        here = seq * 16 + n
        blocks = [block(listed[v, here]) for v in range(VB)]
        blocks += [block(jnp.maximum(here - SLASH + v, 0)) for v in range(SLASH + 1)]
        blocks.append(jnp.zeros((1, 9, 16, 128), jnp.bfloat16))
        return keys_from(jnp.concatenate(blocks, axis=0))

    col = lax.broadcasted_iota(jnp.int32, (BLK, 256), 1)
    row = lax.broadcasted_iota(jnp.int32, (BLK, 256), 0)
    causal = (col >= 128) & (col - 128 <= SLASH * BLK + row)

    def score(n):
        here = seq * 16 + n
        ok = causal & (here - SLASH + (col - 128) // BLK >= 0)
        for v in range(VB):
            ok = ok | ((col // BLK == v) & (listed[v, here] <= here - SLASH - 1))
        bias = jnp.where(ok, 0.0, NEG)
        values, rope = keys_of(n)
        s = dot_t(absorbed[n].reshape(512, 640), jnp.concatenate([values, rope], axis=1))
        return (s.reshape(16, BLK, 256) + bias[None]).reshape(512, 256)

    def weigh(s):
        m = jnp.max(s, axis=1, keepdims=True)
        e = jnp.exp2((s - m) * EXP2)
        return e.astype(jnp.bfloat16), 1.0 / jnp.sum(e, axis=1, keepdims=True)

    def mix(n, e, inverse):
        got = dot(e, keys_of(n)[0]) * inverse
        start = pl.multiple_of(n * BLK, BLK)
        ctx[:, pl.ds(start, BLK), :] = got.astype(jnp.bfloat16).reshape(16, BLK, 512)

    shift = (
        lax.broadcasted_iota(jnp.int32, (128, 128), 0) == lax.broadcasted_iota(jnp.int32, (128, 128), 1) + 64
    ).astype(jnp.float32).astype(jnp.bfloat16)
    group = 3 * UNROLL

    def pages_out(k):
        ropes = []
        for j in range(group):
            i = k * group + j
            which = slots[j % 3, k * UNROLL + j // 3]
            page = block(jnp.maximum(which, 0))[0]
            page = jnp.where(which >= 0, page, jnp.zeros_like(page))
            for r in range(2):
                for w in range(4):
                    paged_hold[i, 16 * r : 16 * r + 16, 128 * w : 128 * w + 128] = page[4 * r + w]
            ropes.append(page[8])
        second = dot(jnp.concatenate(ropes, axis=0), shift).astype(jnp.bfloat16)
        for j in range(group):
            i = k * group + j
            paged_hold[i, :16, 512:576] = ropes[j][:, :64]
            paged_hold[i, 16:, 512:576] = second[16 * j : 16 * j + 16, :64]
        pages_copy(k).start()

    def pages_copy(k):
        part = pl.ds(k * group, group)
        return pltpu.make_async_copy(paged_hold.at[part], paged.at[0, part], s_paged.at[k])

    @pl.loop(0, 16 // UNROLL)
    def _(k):
        turns = [k * UNROLL + u for u in range(UNROLL)]
        scores = [score(n) for n in turns]
        weights = [weigh(s) for s in scores]
        for n, w in zip(turns, weights):
            mix(n, *w)
        pages_out(k)

    in_vu.wait()
    m = jnp.maximum(mine[:, 512:640], theirs[:, 512:640])
    here, there = jnp.exp2((mine[:, 512:640] - m) * EXP2), jnp.exp2((theirs[:, 512:640] - m) * EXP2)
    both = mine[:, 640:] * here + theirs[:, 640:] * there
    decoded = (mine[:, :512] * here[:, :1] + theirs[:, :512] * there[:, :1]) / both[:, :1]
    decoded = decoded.reshape(16, 8, 512).astype(jnp.bfloat16)
    outs = []
    for h in range(16):
        cols = slice(128 * h, 128 * h + 128)
        got = dot(decoded[h], vu[h]).astype(jnp.bfloat16)
        for b in range(4):
            step_out[b, :, cols] = got[2 * b : 2 * b + 2]
        out[:, cols] = dot(ctx[h], vu[h]).astype(jnp.bfloat16)
        if h % 2 == 1:
            wide = slice(128 * (h - 1), 128 * h + 128)
            outs.append(pltpu.make_async_copy(out.at[:, wide], prefill_out.at[:, wide], s_out.at[h // 2]))
            outs[-1].start()
    outs.append(pltpu.make_async_copy(step_out, decode_out, s_out.at[8]))
    outs[-1].start()
    for copy in outs:
        copy.wait()
    for k in range(16 // UNROLL):
        pages_copy(k).wait()


def gather_call(*args):
    vmem, any_ = pl.BlockSpec(memory_space=pltpu.VMEM), pl.BlockSpec(memory_space=pl.ANY)
    smem = pl.BlockSpec(memory_space=pltpu.SMEM)
    bf16, f32, i32 = jnp.bfloat16, jnp.float32, jnp.int32
    dma = pltpu.SemaphoreType.DMA
    args = [pltpu.with_memory_space_constraint(x, pltpu.HBM) for x in args]
    return pl.pallas_call(
        gather_kernel,
        out_shape=(
            pltpu.VMEM((4, 4, 4, 2, 18, 16, 128), bf16),
            pltpu.VMEM((16, 16, BLK, 640), bf16),
            pltpu.VMEM((128, 768), f32),
            pltpu.VMEM((128, 768), f32),
            pltpu.SMEM((4, 256), i32),
            pltpu.SMEM((8, 128), i32),
            pltpu.SMEM((4,), i32),
        ),
        in_specs=[any_] * 10,
        out_specs=(vmem,) * 4 + (smem,) * 3,
        scratch_shapes=[
            pltpu.VMEM((64, 576), bf16),
            pltpu.VMEM((1, 256), i32),
            pltpu.VMEM((4, 2, 2048), bf16),
            pltpu.VMEM((4, 2, 1024), bf16),
            pltpu.VMEM((4, 2, 576), bf16),
            pltpu.VMEM((18, 16, 128), bf16),
            pltpu.VMEM((512, 2048), bf16),
            pltpu.VMEM((512, 1024), bf16),
            pltpu.VMEM((16, 128, 512), bf16),
            pltpu.VMEM((8, 3072), f32),
            pltpu.VMEM((8, 576), f32),
            pltpu.VMEM((16, 8, 640), f32),
            pltpu.VMEM((2, 128, 640), bf16),
            pltpu.VMEM((128, 768), f32),
            pltpu.VMEM((256, 512), f32),
            pltpu.VMEM((256, 128), f32),
            pltpu.VMEM((256, 128), f32),
            pltpu.VMEM((8, 128), i32),
            dma((COPIES + 2,)), dma((COPIES + 2,)), dma((12,)),
        ],
        compiler_params=pltpu.CompilerParams(
            collective_id=0, has_side_effects=True, vmem_limit_bytes=24 << 20
        ),
        cost_estimate=pl.CostEstimate(flops=4 << 30, bytes_accessed=32 << 20, transcendentals=1 << 20),
        name="gather_absorb_decode",
    )(*args)


def attend_call(cache, absorbed, mine, theirs, listed, slots, prefix, value_up):
    vmem, smem, any_ = (pl.BlockSpec(memory_space=m) for m in (pltpu.VMEM, pltpu.SMEM, pl.ANY))
    bf16, f32 = jnp.bfloat16, jnp.float32
    dma = pltpu.SemaphoreType.DMA
    large = [pltpu.with_memory_space_constraint(x, pltpu.VMEM) for x in (cache, absorbed, mine, theirs)]
    small = [pltpu.with_memory_space_constraint(x, pltpu.SMEM) for x in (listed, slots)]
    value_up = pltpu.with_memory_space_constraint(value_up, pltpu.HBM)
    return pl.pallas_call(
        attend_kernel,
        out_shape=(
            jax.ShapeDtypeStruct((512, 2048), bf16),
            jax.ShapeDtypeStruct((1, 48, BLK, 576), bf16),
            jax.ShapeDtypeStruct((4, 2, 2048), bf16),
        ),
        in_specs=[smem] * 2 + [vmem] * 4 + [any_],
        out_specs=(any_, any_, any_),
        scratch_shapes=[
            pltpu.VMEM((16, 512, 128), bf16),
            pltpu.VMEM((16, 512, 512), bf16),
            pltpu.VMEM((512, 2048), bf16),
            pltpu.VMEM((48, BLK, 576), bf16),
            pltpu.VMEM((4, 2, 2048), bf16),
            dma, dma((9,)), dma((4,)),
        ],
        compiler_params=pltpu.CompilerParams(vmem_limit_bytes=24 << 20),
        cost_estimate=pl.CostEstimate(flops=8 << 30, bytes_accessed=20 << 20, transcendentals=3 << 20),
        name="attend",
    )(*small, *large, value_up)


def on_device(
    query_nope, query_rope, latent_cache, key_up, value_up, vertical_lists, page_owner,
    step_nope, step_rope, step_latent, prefix_lengths,
):
    kept = gather_call(
        prefix_lengths, latent_cache, vertical_lists.transpose(0, 2, 1), page_owner.reshape(1, 256),
        step_nope, step_rope, step_latent, query_nope, query_rope, key_up,
    )
    return attend_call(*kept, value_up)


def solution(mesh):
    placed = (
        P("seq", "dec"), P("seq", "dec"), P(("seq", "dec"), None), P("dec", None, None), P("dec", None, None),
        P(), P(), P("seq", None, "dec"), P("seq", None, "dec"), P("seq", None, None), P("seq"),
    )
    return jax.shard_map(
        on_device,
        mesh=mesh,
        in_specs=placed,
        out_specs=(P("seq", "dec"), P("dec", None, None, None), P("seq", None, "dec")),
        check_vma=False,
    )
```
